256 devices in a mesh: expert: 32 (over y, z), tensor: 8 (over x, core).
Axes of the slice: x: 4, y: 4, z: 8, core: 2. Of those that a mesh axis runs over, the one named last changes fastest.
Arguments:
- token_codes: bfloat16 [1024, 5120], P('expert', 'tensor'), may hold values from -448 to 448
- token_scale: bfloat16 [1024, 40], P('expert', 'tensor'), may hold values from 0.0019989014 to 0.019897461
- grad_out: bfloat16 [1024, 5120], P('expert', 'tensor'), may hold values from -0.59765625 to 0.59765625
- expert_ids: int32 [1024, 8], P('expert'), may hold values from 0 to 31, all different within a row; in each aligned block of 32 rows (0 to 31, 32 to 63, ...) at most 12 rows name the same one
- gate_probs: float32 [1024, 8], P('expert'), may hold values from 0.05 to 0.6
- w_in: bfloat16 [32, 2, 1536, 5120], P('expert', None, 'tensor'), may hold values from -0.078125 to 0.078125
- w_in_scale: float32 [32, 2, 1536, 40], P('expert', None, 'tensor'), may hold values from 0.5 to 2
- w_down: bfloat16 [32, 1536, 5120], P('expert', 'tensor'), may hold values from -0.15625 to 0.15625
- w_down_scale: float32 [32, 1536, 40], P('expert', 'tensor'), may hold values from 0.5 to 2
Outputs:
- grad_input: bfloat16 [1024, 5120], P('expert', 'tensor')
- grad_gates: bfloat16 [1024, 8], P('expert')
- grad_w_in: bfloat16 [32, 2, 1536, 5120], P('expert', None, 'tensor')
- grad_w_down: bfloat16 [32, 1536, 5120], P('expert', 'tensor')
The draws below stay inside these ranges and needn't reach their ends.
Inputs may be any that keep to these rules, and one draw needn't show every extreme that they name: `expert_ids`: each row names 8 different experts. Among the 32 rows of one index of expert, no expert is named by more than 12 rows, a bound that some block reaches.
All inputs are finite; a program needn't handle non-finite values.
Results may differ from the reference program's by a relative error of at most 0.02.
Values may be sent and summed in bfloat16 or wider, within the bound.
A program may use at most 128 MiB of HBM per device.

```python
import math
import jax
import jax.numpy as jnp
import numpy as np
from jax import lax

D = 5120
FF = 1536
TOP = 8
EXPERTS = 32
BLOCK = 128
TOK_DEV = 32
CAP = 12
TOKENS = 1024
N_EXPERT = 32
N_TENSOR = 8


def level_of(stream_key, shape, pieces, smallest, largest):
    loudness, own = 1.0, jax.random.fold_in(stream_key, 6)
    for position, shards_of in pieces:
        draws = jnp.exp(jax.random.uniform(jax.random.fold_in(own, position), (shards_of,), jnp.float32, smallest / len(pieces), largest / len(pieces)))
        loudness = loudness * jnp.repeat(draws, shape[position] // shards_of).reshape([-1 if axis == position else 1 for axis in range(len(shape))])
    return loudness


def shared_out(rng, own, number, rows, count, top, bound, slope):
    ranking = jax.random.permutation(rng, count)
    crowded, common = load_shares(count, rows * top, bound, slope, True), load_shares(count, rows * top, bound, slope, False)
    places = jnp.arange(count)

    def named(sizes, turn):
        used = int((sizes > 0).sum())
        fixed = max(1, used // 4)
        passed = fixed + (places - fixed + turn * (used - fixed)) % max(1, count - fixed)
        return jnp.zeros((count,), jnp.int32).at[ranking[jnp.where(places < fixed, places, passed)]].set(jnp.asarray(sizes, jnp.int32))

    sizes = jnp.where(number % 4 == 0, named(crowded, number // 4), named(common, number - number // 4 - 1))
    mixed = jax.random.permutation(jax.random.fold_in(own, 3), count)
    source_of, taker = mixed[0:count // 2 * 2:2], mixed[1:count // 2 * 2:2]
    margin = jnp.minimum(sizes[source_of] - 1, bound - sizes[taker]) // 2
    margin = jnp.where((source_of == ranking[0]) | (taker == ranking[0]) | (sizes[taker] == 0), 0, jnp.maximum(margin, 0))
    passed = jax.random.randint(jax.random.fold_in(own, 4), (count // 2,), 0, 1 << 20) % (margin + 1)
    sizes = sizes.at[source_of].add(-passed).at[taker].add(passed)
    members = jnp.searchsorted(jnp.cumsum(sizes), jnp.arange(rows * top), side="right").astype(jnp.int32)
    listing = members.reshape(top, rows).T
    listing = listing[jax.random.permutation(jax.random.fold_in(own, 1), rows)]
    turn = jax.random.randint(jax.random.fold_in(own, 2), (rows, 1), 0, top)
    return jnp.take_along_axis(listing, (jnp.arange(top)[None, :] + turn) % top, axis=1)


def load_shares(number_of, total, reach, skew, full):
    portions = [(1 << 20) // math.isqrt(standing ** skew) + 1 for standing in range(1, number_of + 1)]
    largest = reach if full else min(reach, max(-(-total // number_of), total * portions[0] // sum(portions)))
    least = 1 if total - largest >= number_of - 1 else 0
    given, spare = [largest] + [least] * (number_of - 1), total - largest - least * (number_of - 1)
    while spare > 0:
        movable = [i for i in range(1, number_of) if given[i] < largest] or [i for i in range(1, number_of) if given[i] < reach]
        whole, left = sum([portions[i] for i in movable]), spare
        for i in movable:
            addition = min(reach - given[i], max(1, left * portions[i] // whole), spare)
            given[i] = given[i] + addition
            spare = spare - addition
    return np.array(given)


def centred(key, extent, spread, bound, pieces=(), kind=jnp.bfloat16):
    drawn = spread * jax.random.normal(key, extent, jnp.float32)
    if pieces:
        drawn = drawn * level_of(key, extent, pieces, -0.22, 0.18)
    return jnp.clip(drawn, -bound, bound).astype(kind)


def setup_inputs(seed: int = 0) -> dict:
    key_of = jax.random.split(jax.random.key(seed), 10)
    token_codes = centred(key_of[0], (TOKENS, D), 150.0, 448.0, ((0, 32), (1, 8)))
    token_scale = jnp.clip(jnp.exp(math.log(0.019897461) - 2.2979944 * jax.random.uniform(key_of[1], (TOKENS, D // BLOCK), jnp.float32) ** level_of(key_of[1], (TOKENS, D // BLOCK), ((0, 32), (1, 8)), -0.2, 0.2)), 0.0019989014, 0.019897461).astype(jnp.bfloat16)
    grad_out = centred(key_of[2], (TOKENS, D), 0.1, 0.59765625, ((0, 32), (1, 8)))
    expert_ids_keys = jax.random.split(jax.random.fold_in(key_of[3], 1), TOKENS // TOK_DEV)
    expert_ids_turns = jax.random.permutation(jax.random.fold_in(key_of[3], 3), TOKENS // TOK_DEV)
    expert_ids = jax.vmap(lambda own, number: shared_out(jax.random.fold_in(key_of[3], 2), own, number, TOK_DEV, EXPERTS, TOP, CAP, 2))(expert_ids_keys, expert_ids_turns).reshape((TOKENS, TOP))
    gate_probs = jnp.clip(0.05 + 0.55 * jax.random.uniform(key_of[4], (TOKENS, TOP), jnp.float32) ** level_of(key_of[4], (TOKENS, TOP), ((0, 32),), -0.2, 0.2), 0.05, 0.6)
    w_in = centred(key_of[5], (EXPERTS, 2, FF, D), D ** -0.5, 0.078125, ((0, 32), (2, 8)))
    w_in_scale = jnp.clip(jnp.exp(math.log(2.0) - 1.3862944 * jax.random.uniform(key_of[6], (EXPERTS, 2, FF, D // BLOCK), jnp.float32) ** level_of(key_of[6], (EXPERTS, 2, FF, D // BLOCK), ((0, 32), (2, 8)), -0.2, 0.2)), 0.5, 2.0)
    w_down = centred(key_of[7], (EXPERTS, FF, D), FF ** -0.5, 0.15625, ((0, 32), (1, 8)))
    w_down_scale = jnp.clip(jnp.exp(math.log(2.0) - 1.3862944 * jax.random.uniform(key_of[8], (EXPERTS, FF, D // BLOCK), jnp.float32) ** level_of(key_of[8], (EXPERTS, FF, D // BLOCK), ((0, 32), (1, 8)), -0.2, 0.2)), 0.5, 2.0)
    return {"token_codes": token_codes, "token_scale": token_scale, "grad_out": grad_out, "expert_ids": expert_ids, "gate_probs": gate_probs, "w_in": w_in, "w_in_scale": w_in_scale, "w_down": w_down, "w_down_scale": w_down_scale}


def reference(token_codes, token_scale, grad_out, expert_ids, gate_probs, w_in, w_in_scale, w_down, w_down_scale):
    code_blocks = token_codes.astype(jnp.float32).reshape(TOKENS, D // BLOCK, BLOCK)
    x_rows = (code_blocks * token_scale.astype(jnp.float32)[:, :, None]).astype(jnp.bfloat16).reshape(TOKENS, D)
    routed = expert_ids.reshape(-1).astype(jnp.int32)
    rows_most = N_EXPERT * CAP
    group_width = FF // N_TENSOR
    x_padded = jnp.concatenate([x_rows, jnp.zeros((1, D), jnp.bfloat16)], axis=0)
    grad_padded = jnp.concatenate([grad_out, jnp.zeros((1, D), jnp.bfloat16)], axis=0)
    prob_padded = jnp.concatenate([gate_probs.astype(jnp.bfloat16).reshape(-1), jnp.zeros((1,), jnp.bfloat16)], axis=0)

    def one_expert(expert):
        slot_index = jnp.nonzero(routed == expert, size=rows_most, fill_value=TOKENS * TOP)[0].astype(jnp.int32)
        token_index = jnp.minimum(slot_index // TOP, TOKENS).astype(jnp.int32)
        row_values = jnp.take(x_padded, token_index, axis=0)
        grad_rows = jnp.take(grad_padded, token_index, axis=0)
        prob_column = jnp.take(prob_padded, slot_index, axis=0).astype(jnp.float32)[:, None]
        in_grouped = w_in[expert].astype(jnp.float32).reshape(2, FF, D // BLOCK, BLOCK)
        w_pair = (in_grouped * w_in_scale[expert][:, :, :, None]).astype(jnp.bfloat16).reshape(2, FF, D)
        down_grouped = w_down[expert].astype(jnp.float32).reshape(FF, D // BLOCK, BLOCK)
        w_out = (down_grouped * w_down_scale[expert][:, :, None]).astype(jnp.bfloat16).reshape(FF, D)
        gate_pre = jnp.dot(row_values, w_pair[0].T, preferred_element_type=jnp.float32)
        up_pre = jnp.dot(row_values, w_pair[1].T, preferred_element_type=jnp.float32)
        hidden_grad = jnp.dot(grad_rows, w_out.T, preferred_element_type=jnp.float32)
        gate_sig = jax.nn.sigmoid(gate_pre)
        gate_act = gate_pre * gate_sig
        gate_rows = jnp.sum(hidden_grad * gate_act * up_pre, axis=1).astype(jnp.bfloat16)
        gate_full = hidden_grad * up_pre * gate_sig * (1.0 + gate_pre * (1.0 - gate_sig))
        up_full = hidden_grad * gate_act
        gate_grad = gate_full.astype(jnp.bfloat16)
        up_grad = up_full.astype(jnp.bfloat16)
        partials = jnp.einsum("mjf,jfd->jmd", gate_grad.astype(jnp.float32).reshape(rows_most, N_TENSOR, group_width),
                              w_pair[0].astype(jnp.float32).reshape(N_TENSOR, group_width, D))
        partials = partials + jnp.einsum("mjf,jfd->jmd", up_grad.astype(jnp.float32).reshape(rows_most, N_TENSOR, group_width),
                                         w_pair[1].astype(jnp.float32).reshape(N_TENSOR, group_width, D))
        rounded = lax.optimization_barrier(partials.astype(jnp.bfloat16))
        slot_rows = jnp.sum(rounded.astype(jnp.float32), axis=0).astype(jnp.bfloat16)
        gate_weighted = (prob_column * gate_full).astype(jnp.bfloat16)
        up_weighted = (prob_column * up_full).astype(jnp.bfloat16)
        hidden_act = (prob_column * gate_act * up_pre).astype(jnp.bfloat16)
        grad_gate_w = jnp.dot(gate_weighted.T, row_values, preferred_element_type=jnp.float32)
        grad_up_w = jnp.dot(up_weighted.T, row_values, preferred_element_type=jnp.float32)
        grad_pair = jnp.stack([grad_gate_w, grad_up_w], axis=0).astype(jnp.bfloat16)
        grad_down = jnp.dot(hidden_act.T, grad_rows, preferred_element_type=jnp.float32).astype(jnp.bfloat16)
        return slot_index, slot_rows, gate_rows, grad_pair, grad_down

    slot_index, slot_rows, gate_rows, grad_w_in, grad_w_down = lax.map(one_expert, jnp.arange(EXPERTS, dtype=jnp.int32))
    slot_index = slot_index.reshape(-1)
    slot_grad = jnp.zeros((TOKENS * TOP + 1, D), jnp.bfloat16).at[slot_index].set(slot_rows.reshape(-1, D))
    slot_grad = slot_grad[:TOKENS * TOP].reshape(TOKENS, TOP, D)
    gate_slots = jnp.zeros((TOKENS * TOP + 1,), jnp.bfloat16).at[slot_index].set(gate_rows.reshape(-1))
    grad_gates = gate_slots[:TOKENS * TOP].reshape(TOKENS, TOP)
    grad_input = jnp.einsum("tkd,tk->td", slot_grad.astype(jnp.float32), gate_probs.astype(jnp.float32)).astype(jnp.bfloat16)
    return grad_input, grad_gates, grad_w_in, grad_w_down
```

```python
import functools

import jax
import jax.numpy as jnp
from jax import lax
from jax.experimental import pallas as pl
from jax.experimental.pallas import tpu as pltpu
from jax.sharding import PartitionSpec as P

MESH = pl.DeviceIdType.MESH
BLOCK = 128
CAP = 12
PAD = 16
NX, NY, NZ = 4, 4, 8
NE = NY * NZ
TOK = 32
TOP = 8
WL = 640
WIDTH = 5120
HID = 192
ROWS = NE * CAP
CH = NZ * CAP
CHP = NZ * PAD
RS = CH + 16
HALF = CH // 2
F32 = jnp.float32
BF16 = jnp.bfloat16


def mm(a, b, dims):
    return lax.dot_general(a, b, (dims, ((), ())), preferred_element_type=F32)


def iota(shape, axis):
    return lax.broadcasted_iota(jnp.int32, shape, axis)


def onehot(mask):
    return jnp.where(mask, 1.0, 0.0).astype(BF16)


def exchange(
    ids_t, prob_t, ids, codes, tok_scale, grad_out, in_scale, down_scale, w_in, w_down,
    gi_out, gg_out, hid_out, rows_out,
    send, recv, own, rows, weights, parts, core_in, far_sum, plus_sum, minus_sum,
    relay_a, relay_b, from_minus, from_plus, back_send, back_recv, chosen, prob_col,
    sem_w, sem_own, sem_out, a_s, a_r, g_s, g_r, r_s, r_r, b_s, b_r,
):
    er = lax.axis_index("expert")
    te = lax.axis_index("tensor")
    y, z = lax.div(er, NZ), lax.rem(er, NZ)
    x, core = lax.div(te, 2), lax.rem(te, 2)
    other = 1 - core
    x_plus, x_minus, x_far = lax.rem(x + 1, NX), lax.rem(x + 3, NX), lax.rem(x + 2, NX)
    t_plus, t_minus, t_far = x_plus * 2 + core, x_minus * 2 + core, x_far * 2 + core
    t_core = x * 2 + other

    def ahead(rel):
        dy, dz = lax.div(rel, NZ), lax.rem(rel, NZ)
        return lax.rem(y + dy, NY) * NZ + lax.rem(z + dz, NZ)

    def behind(rel):
        dy, dz = lax.div(rel, NZ), lax.rem(rel, NZ)
        return lax.rem(y + NY - dy, NY) * NZ + lax.rem(z + NZ - dz, NZ)

    barrier = pltpu.get_barrier_semaphore()

    @pl.loop(1, NE)
    def _(rel):
        pl.semaphore_signal(barrier, inc=1, device_id=(ahead(rel), te), device_id_type=MESH)

    for peer in (t_plus, t_minus, t_core):
        pl.semaphore_signal(barrier, inc=1, device_id=(er, peer), device_id_type=MESH)

    load_in = pltpu.make_async_copy(w_in, weights.at[pl.ds(0, 2 * HID), :], sem_w.at[0])
    load_down = pltpu.make_async_copy(w_down, weights.at[pl.ds(2 * HID, HID), :], sem_w.at[1])
    load_in.start()
    load_down.start()

    slot = iota((NE * PAD, 128), 0)
    rel_of = slot >> 4
    r_of = slot & 15
    expert_of = ((y + (rel_of >> 3)) & 3) * NZ + ((z + (rel_of & 7)) & 7)
    weight = jnp.zeros((NE * PAD, 128), F32)
    for k in range(TOP):
        weight = weight + jnp.where(ids_t[k : k + 1, :] == expert_of, prob_t[k : k + 1, :], 0.0)
    before = onehot(iota((128, 128), 0) < iota((128, 128), 1))
    place = mm(onehot(weight > 0.0), before, ((1,), (0,)))
    mine = jnp.logical_and(weight > 0.0, place == r_of.astype(F32))
    pick = onehot(mine)[:, :TOK]
    kept = jnp.where(mine, weight, 0.0)
    kept_high = kept.astype(BF16)
    chosen[0] = kept_high
    chosen[1] = (kept - kept_high.astype(F32)).astype(BF16)
    for j in range(WL // BLOCK):
        cols = slice(j * BLOCK, (j + 1) * BLOCK)
        values = (codes[:, cols].astype(F32) * tok_scale[:, j : j + 1].astype(F32)).astype(BF16)
        packed = mm(pick, values, ((1,), (0,)))
        if j == 0:
            packed = packed + jnp.where(r_of == CAP, weight, 0.0)
        send[:, cols] = packed.astype(BF16)
    send[:, WL:] = mm(pick, grad_out[...], ((1,), (0,))).astype(BF16)
    recv[0:PAD, :] = send[0:PAD, :]

    pl.semaphore_wait(barrier, NE - 1 + 3)

    def at16(ref, rel):
        return ref.at[pl.ds(pl.multiple_of(rel * PAD, PAD), PAD), :]

    def out_copy(rel):
        return pltpu.make_async_remote_copy(
            src_ref=at16(send, rel), dst_ref=at16(recv, rel), send_sem=a_s.at[rel], recv_sem=a_r.at[rel],
            device_id=(ahead(rel), te), device_id_type=MESH,
        )

    def back_copy(rel):
        return pltpu.make_async_remote_copy(
            src_ref=at16(back_send, rel), dst_ref=at16(back_recv, rel), send_sem=b_s.at[rel], recv_sem=b_r.at[rel],
            device_id=(behind(rel), te), device_id_type=MESH,
        )

    @pl.loop(1, NE)
    def _(rel):
        out_copy(rel).start()

    def cols_of(t):
        return pl.ds(pl.multiple_of(t * WL, BLOCK), WL)

    def window(c, t, first=0, count=CH):
        return rows.at[:, pl.ds(pl.multiple_of(c * CH + first, 16), count), cols_of(t)]

    def own_rows(c):
        return own.at[:, pl.ds(pl.multiple_of(c * CH, 16), CH), :]

    def own_copy(c):
        return pltpu.make_async_copy(own_rows(c), window(c, te), sem_own.at[c])

    def gather_copy(c, k):
        ref, peer = (
            (lambda: window(c, te), t_plus),
            (lambda: window(c, te), t_minus),
            (lambda: window(c, te), t_core),
            (lambda: window(c, t_minus, 0, HALF), t_plus),
            (lambda: window(c, t_plus, HALF, HALF), t_minus),
            (lambda: window(c, t_minus), t_core),
            (lambda: window(c, t_plus), t_core),
            (lambda: window(c, t_far), t_core),
        )[k]
        ref = ref()
        return pltpu.make_async_remote_copy(
            src_ref=own_rows(c) if k < 3 else ref, dst_ref=ref, send_sem=g_s.at[k, c], recv_sem=g_r.at[k, c],
            device_id=(er, peer), device_id_type=MESH,
        )

    to_core = (x_far * 2 + other, x_plus * 2 + other, x_minus * 2 + other, t_core)

    def sum_copy(c, k):
        if k < 4:
            src, dst, peer = parts.at[c, :, cols_of(to_core[k])], core_in.at[k, c], t_core
        elif k == 4:
            src, dst, peer = far_sum.at[c, pl.ds(0, HALF), :], relay_a.at[c], t_plus
        elif k == 5:
            src, dst, peer = far_sum.at[c, pl.ds(HALF, RS - HALF), :], relay_b.at[c], t_minus
        elif k == 6:
            src, dst, peer = plus_sum.at[c], from_minus.at[c], t_plus
        else:
            src, dst, peer = minus_sum.at[c], from_plus.at[c], t_minus
        return pltpu.make_async_remote_copy(
            src_ref=src, dst_ref=dst, send_sem=r_s.at[k, c], recv_sem=r_r.at[k, c],
            device_id=(er, peer), device_id_type=MESH,
        )

    def rows_copy(c):
        span = pl.ds(pl.multiple_of(c * CH, 16), CH)
        return pltpu.make_async_copy(rows.at[:, span, :], rows_out.at[:, span, :], sem_out.at[c])

    load_in.wait()
    load_down.wait()

    def scale_rows(scale_ref, first, count):
        @pl.loop(0, count // 16)
        def _(i):
            at = pl.ds(pl.multiple_of(i * 16, 16), 16)
            to = pl.ds(pl.multiple_of(first + i * 16, 16), 16)
            scale = scale_ref[at, :]
            for q in range(WIDTH // BLOCK):
                cols = slice(q * BLOCK, (q + 1) * BLOCK)
                weights[to, cols] = (weights[to, cols].astype(F32) * scale[:, q : q + 1]).astype(BF16)

    scale_rows(in_scale, 0, 2 * HID)
    scale_rows(down_scale, 2 * HID, HID)

    def dispatch_stage(c):
        @pl.loop(0, NZ)
        def _(i):
            rel = c * NZ + i

            @pl.when(rel > 0)
            def _():
                out_copy(rel).wait_recv()

        row = iota((CH, CHP), 0)
        col = iota((CH, CHP), 1)
        group = lax.div(row, CAP)
        within = row - group * CAP
        squeeze = onehot(col == group * PAD + within)
        span = pl.ds(pl.multiple_of(c * CH, 16), CH)
        part = pl.ds(pl.multiple_of(c * CHP, CHP), CHP)
        own[0, span, :] = mm(squeeze, recv[part, :WL], ((1,), (0,))).astype(BF16)
        own[1, span, :] = mm(squeeze, recv[part, WL:], ((1,), (0,))).astype(BF16)
        own_copy(c).start()
        for k in (0, 1, 2):
            gather_copy(c, k).start()
        named = mm(onehot(col == group * PAD + CAP), recv[part, :BLOCK], ((1,), (0,)))
        rank = mm(onehot(named > 0.0), before, ((1,), (0,)))
        taken = jnp.logical_and(named > 0.0, rank == within.astype(F32))
        prob_col[span, :] = jnp.sum(jnp.where(taken, named, 0.0), axis=1, keepdims=True)

    def relay_stage(c):
        gather_copy(c, 0).wait_recv()
        gather_copy(c, 3).start()
        gather_copy(c, 5).start()
        gather_copy(c, 1).wait_recv()
        gather_copy(c, 4).start()
        gather_copy(c, 6).start()

    def far_stage(c):
        gather_copy(c, 3).wait_recv()
        gather_copy(c, 4).wait_recv()
        gather_copy(c, 7).start()

    def compute_stage(c):
        for k in (2, 5, 6, 7):
            gather_copy(c, k).wait_recv()
        own_copy(c).wait()
        rows_copy(c).start()
        span = pl.ds(pl.multiple_of(c * CH, 16), CH)
        row_values = rows[0, span, :]
        gate = mm(row_values, weights[0:HID, :], ((1,), (1,)))
        up = mm(row_values, weights[HID : 2 * HID, :], ((1,), (1,)))
        hidden = mm(rows[1, span, :], weights[2 * HID :, :], ((1,), (1,)))
        sig = jax.nn.sigmoid(gate)
        act = gate * sig
        gate_full = hidden * up * sig * (1.0 + gate * (1.0 - sig))
        up_full = hidden * act
        gate_grad = gate_full.astype(BF16)
        up_grad = up_full.astype(BF16)
        acted = act * up
        share = hidden * acted
        share_high = share.astype(BF16)
        ones = jnp.ones((16, HID), BF16)
        gate_row = mm(ones, share_high, ((1,), (1,))) + mm(
            ones, (share - share_high.astype(F32)).astype(BF16), ((1,), (1,))
        )
        gate_row = gate_row.astype(BF16)
        for t in range(2 * NX):
            cols = slice(t * WL, (t + 1) * WL)
            part = mm(gate_grad, weights[0:HID, cols], ((1,), (0,)))
            part = part + mm(up_grad, weights[HID : 2 * HID, cols], ((1,), (0,)))
            parts[c, 0:CH, cols] = part.astype(BF16)
            parts[c, CH:RS, cols] = jnp.zeros((16, WL), BF16)
            parts[c, CH:RS, t * WL : t * WL + CH] = gate_row
        for k in range(4):
            sum_copy(c, k).start()
        prob = prob_col[span, :]
        hid_out[0, span, :] = (prob * gate_full).astype(BF16)
        hid_out[1, span, :] = (prob * up_full).astype(BF16)
        hid_out[2, span, :] = (prob * acted).astype(BF16)

    def chip_sum(c, k, t):
        return parts[c, :, cols_of(t)].astype(F32) + core_in[k, c].astype(F32)

    def core_stage(c):
        sum_copy(c, 0).wait_recv()
        far_sum[c] = chip_sum(c, 0, t_far).astype(BF16)
        sum_copy(c, 4).start()
        sum_copy(c, 5).start()

    def ring_stage(c):
        sum_copy(c, 1).wait_recv()
        total = chip_sum(c, 1, t_plus)
        sum_copy(c, 4).wait_recv()
        plus_sum[c, 0:HALF, :] = (total[0:HALF] + relay_a[c].astype(F32)).astype(BF16)
        plus_sum[c, HALF:RS, :] = total[HALF:RS].astype(BF16)
        sum_copy(c, 6).start()
        sum_copy(c, 2).wait_recv()
        total = chip_sum(c, 2, t_minus)
        sum_copy(c, 5).wait_recv()
        minus_sum[c, 0:HALF, :] = total[0:HALF].astype(BF16)
        minus_sum[c, HALF:RS, :] = (total[HALF:RS] + relay_b[c].astype(F32)).astype(BF16)
        sum_copy(c, 7).start()

    def return_stage(c):
        sum_copy(c, 3).wait_recv()
        total = chip_sum(c, 3, te)
        sum_copy(c, 6).wait_recv()
        sum_copy(c, 7).wait_recv()
        total = total + from_minus[c].astype(F32) + from_plus[c].astype(F32)
        row = iota((CHP, CH), 0)
        col = iota((CHP, CH), 1)
        spread = onehot(jnp.logical_and((row & 15) < CAP, col == (row >> 4) * CAP + (row & 15)))
        out = mm(spread, total[0:CH].astype(BF16), ((1,), (0,)))
        r = iota((CHP, WL), 0) & 15
        out = out + jnp.where(r == CAP, total[CH : CH + 1, :], 0.0)
        at = pl.ds(pl.multiple_of(c * CHP, CHP), CHP)
        back_send[at, :] = out.astype(BF16)

        @pl.loop(0, NZ)
        def _(i):
            rel = c * NZ + i

            @pl.when(rel > 0)
            def _():
                back_copy(rel).start()

    stages = (
        (dispatch_stage, 0), (relay_stage, 1), (far_stage, 2), (compute_stage, 3),
        (core_stage, 4), (ring_stage, 5), (return_stage, 6),
    )

    @pl.loop(0, NY + 6)
    def _(s):
        for stage, lag in stages:

            @pl.when(jnp.logical_and(s >= lag, s < NY + lag))
            def _():
                stage(s - lag)

    back_recv[0:PAD, :] = back_send[0:PAD, :]
    lane = iota((TOK, 128), 1)
    named = jnp.zeros((TOK, 128), F32)
    for k in range(TOP):
        named = named + jnp.where(ids[:, k : k + 1] == lane, 1.0, 0.0)
    earlier = onehot(iota((TOK, TOK), 1) < iota((TOK, TOK), 0))
    rank = mm(earlier, named.astype(BF16), ((1,), (0,)))

    @pl.loop(1, NE)
    def _(rel):
        back_copy(rel).wait_recv()

    arrived = back_recv[...]
    total = mm(chosen[0], arrived, ((0,), (0,))) + mm(chosen[1], arrived, ((0,), (0,)))
    gi_out[...] = total[0:TOK, :].astype(BF16)
    wide = iota((TOK, NE * PAD), 1)
    gates = arrived[:, 0:128]
    for k in range(TOP):
        expert = ids[:, k : k + 1]
        position = jnp.sum(jnp.where(expert == lane, rank, 0.0), axis=1, keepdims=True)
        rel = (((expert >> 3) - y) & 3) * NZ + (((expert & 7) - z) & 7)
        line = mm(onehot(wide == rel * PAD + CAP), gates, ((1,), (0,)))
        spot = ((rel & 7) * CAP).astype(F32) + position
        gg_out[:, k : k + 1] = jnp.sum(
            jnp.where(lane.astype(F32) == spot, line, 0.0), axis=1, keepdims=True
        ).astype(BF16)

    @pl.loop(1, NE)
    def _(rel):
        out_copy(rel).wait_send()
        back_copy(rel).wait_send()

    @pl.loop(0, NY)
    def _(c):
        for k in range(8):
            gather_copy(c, k).wait_send()
            sum_copy(c, k).wait_send()
        rows_copy(c).wait()


def weight_grads(hid, rows, grad_in, grad_down):
    x_rows = rows[0]
    grad_in[0, 0] = mm(hid[0], x_rows, ((0,), (0,))).astype(BF16)
    grad_in[0, 1] = mm(hid[1], x_rows, ((0,), (0,))).astype(BF16)
    grad_down[0] = mm(hid[2], rows[1], ((0,), (0,))).astype(BF16)


def on_device(
    token_codes, token_scale, grad_out, expert_ids, gate_probs, w_in, w_in_scale, w_down, w_down_scale
):
    ids_t = jnp.pad(expert_ids.T, ((0, 0), (0, 128 - TOK)), constant_values=-1)
    prob_t = jnp.pad(gate_probs.T, ((0, 0), (0, 128 - TOK)))
    vmem = pl.BlockSpec(memory_space=pltpu.VMEM)
    hbm = pl.BlockSpec(memory_space=pl.ANY)
    dma = pltpu.SemaphoreType.DMA
    grad_input, grad_gates, hid, rows = pl.pallas_call(
        exchange,
        out_shape=(
            jax.ShapeDtypeStruct((TOK, WL), BF16),
            jax.ShapeDtypeStruct((TOK, TOP), BF16),
            jax.ShapeDtypeStruct((3, ROWS, HID), BF16),
            jax.ShapeDtypeStruct((2, ROWS, WIDTH), BF16),
        ),
        in_specs=[vmem] * 8 + [hbm] * 2,
        out_specs=(vmem, vmem, vmem, hbm),
        scratch_shapes=[
            pltpu.VMEM((NE * PAD, 2 * WL), BF16),
            pltpu.VMEM((NE * PAD, 2 * WL), BF16),
            pltpu.VMEM((2, ROWS, WL), BF16),
            pltpu.VMEM((2, ROWS, WIDTH), BF16),
            pltpu.VMEM((3 * HID, WIDTH), BF16),
            pltpu.VMEM((NY, RS, WIDTH), BF16),
            pltpu.VMEM((4, NY, RS, WL), BF16),
            pltpu.VMEM((NY, RS, WL), BF16),
            pltpu.VMEM((NY, RS, WL), BF16),
            pltpu.VMEM((NY, RS, WL), BF16),
            pltpu.VMEM((NY, HALF, WL), BF16),
            pltpu.VMEM((NY, RS - HALF, WL), BF16),
            pltpu.VMEM((NY, RS, WL), BF16),
            pltpu.VMEM((NY, RS, WL), BF16),
            pltpu.VMEM((NE * PAD, WL), BF16),
            pltpu.VMEM((NE * PAD, WL), BF16),
            pltpu.VMEM((2, NE * PAD, 128), BF16),
            pltpu.VMEM((ROWS, 1), F32),
            dma((2,)),
            dma((NY,)),
            dma((NY,)),
            dma((NE,)),
            dma((NE,)),
            dma((8, NY)),
            dma((8, NY)),
            dma((8, NY)),
            dma((8, NY)),
            dma((NE,)),
            dma((NE,)),
        ],
        compiler_params=pltpu.CompilerParams(
            collective_id=0, has_side_effects=True, vmem_limit_bytes=56 * 1024 * 1024
        ),
    )(
        ids_t, prob_t, expert_ids, token_codes, token_scale, grad_out,
        w_in_scale.reshape(2 * HID, WIDTH // BLOCK), w_down_scale.reshape(HID, WIDTH // BLOCK),
        w_in.reshape(2 * HID, WIDTH), w_down.reshape(HID, WIDTH),
    )
    grad_w_in, grad_w_down = pl.pallas_call(
        weight_grads,
        grid=(WIDTH // WL,),
        in_specs=[
            pl.BlockSpec((3, ROWS, HID), lambda i: (0, 0, 0)),
            pl.BlockSpec((2, ROWS, WL), lambda i: (0, 0, i)),
        ],
        out_specs=(
            pl.BlockSpec((1, 2, HID, WL), lambda i: (0, 0, 0, i)),
            pl.BlockSpec((1, HID, WL), lambda i: (0, 0, i)),
        ),
        out_shape=(
            jax.ShapeDtypeStruct((1, 2, HID, WIDTH), BF16),
            jax.ShapeDtypeStruct((1, HID, WIDTH), BF16),
        ),
        compiler_params=pltpu.CompilerParams(vmem_limit_bytes=56 * 1024 * 1024),
    )(hid, rows)
    return (grad_input, grad_gates, grad_w_in, grad_w_down)


def solution(mesh):
    placed = (
        P("expert", "tensor"),
        P("expert", "tensor"),
        P("expert", "tensor"),
        P("expert", None),
        P("expert", None),
        P("expert", None, "tensor", None),
        P("expert", None, "tensor", None),
        P("expert", "tensor", None),
        P("expert", "tensor", None),
    )
    return jax.shard_map(
        on_device,
        mesh=mesh,
        in_specs=placed,
        out_specs=(
            P("expert", "tensor"),
            P("expert", None),
            P("expert", None, "tensor", None),
            P("expert", "tensor", None),
        ),
        check_vma=False,
    )
```

```python
import functools

import jax
import jax.numpy as jnp
from jax import lax
from jax.experimental import pallas as pl
from jax.experimental.pallas import tpu as pltpu
from jax.sharding import PartitionSpec as P

MESH = pl.DeviceIdType.MESH
BLOCK = 128
CAP = 12
PAD = 16
NX, NY, NZ = 4, 4, 8
NE = NY * NZ
TOK = 32
TOP = 8
WL = 640
WIDTH = 5120
HID = 192
ROWS = NE * CAP
CH = NZ * CAP
CHP = NZ * PAD
HALF = CH // 2
OUT_W = 4 * 256
BACK_W = 4 * 128
RELAYED = (2, 3)
WAY = NZ - 2
STEP = 512
PART = 48
STEPS = 3 * HID // 16 // NY
F32 = jnp.float32
BF16 = jnp.bfloat16


def mm(a, b, dims):
    return lax.dot_general(a, b, (dims, ((), ())), preferred_element_type=F32)


def iota(shape, axis):
    return lax.broadcasted_iota(jnp.int32, shape, axis)


def onehot(mask):
    return jnp.where(mask, 1.0, 0.0).astype(BF16)


def exchange(
    ids_t, prob_t, codes, tok_scale, grad_out, in_scale, down_scale, w_in, w_down,
    gi_out, gg_out, rows, grads,
    payload, scales, send, recv, passing, own, weights, parts, kept_parts, core_in, gate_own, gate_core, gate_chip, gate_in, hid, far_sum, plus_sum, minus_sum,
    relay_a, relay_b, from_minus, from_plus, back_send, back_recv, chosen, gate_pick, gate_spot, prob_col,
    sem_w, sem_own, a_s, a_r, p_s, p_r, g_s, g_r, r_s, r_r, b_s, b_r,
):
    er = lax.axis_index("expert")
    te = lax.axis_index("tensor")
    y, z = lax.div(er, NZ), lax.rem(er, NZ)
    x, core = lax.div(te, 2), lax.rem(te, 2)
    other = 1 - core
    x_plus, x_minus, x_far = lax.rem(x + 1, NX), lax.rem(x + 3, NX), lax.rem(x + 2, NX)
    t_plus, t_minus, t_far = x_plus * 2 + core, x_minus * 2 + core, x_far * 2 + core
    t_core = x * 2 + other

    def ahead(rel):
        dy, dz = lax.div(rel, NZ), lax.rem(rel, NZ)
        return lax.rem(y + dy, NY) * NZ + lax.rem(z + dz, NZ)

    def behind(rel):
        dy, dz = lax.div(rel, NZ), lax.rem(rel, NZ)
        return lax.rem(y + NY - dy, NY) * NZ + lax.rem(z + NZ - dz, NZ)

    barrier = pltpu.get_barrier_semaphore()

    @pl.loop(1, NE)
    def _(rel):
        pl.semaphore_signal(barrier, inc=1, device_id=(ahead(rel), te), device_id_type=MESH)

    for peer in (t_plus, t_minus, t_core, t_far):
        pl.semaphore_signal(barrier, inc=1, device_id=(er, peer), device_id_type=MESH)

    load_in = pltpu.make_async_copy(w_in, weights.at[pl.ds(0, 2 * HID), :], sem_w.at[0])
    load_down = pltpu.make_async_copy(w_down, weights.at[pl.ds(2 * HID, HID), :], sem_w.at[1])
    load_in.start()
    load_down.start()

    eye = onehot(iota((TOK, TOK), 0) == iota((TOK, TOK), 1))
    before = onehot(iota((TOK, TOK), 0) < iota((TOK, TOK), 1))
    tok_cols = mm(eye, tok_scale[...], ((1,), (1,)))
    for j in range(WL // BLOCK):
        cols = slice(j * BLOCK, (j + 1) * BLOCK)
        payload[:, cols] = (codes[:, cols].astype(F32) * tok_cols[:, j : j + 1]).astype(BF16)
    payload[:, WL:] = grad_out[...]

    slot = iota((NE * PAD, TOK), 0)
    rel_of = slot >> 4
    r_of = slot & 15
    expert_of = ((y + (rel_of >> 3)) & 3) * NZ + ((z + (rel_of & 7)) & 7)
    weight = jnp.zeros((NE * PAD, TOK), F32)
    for k in range(TOP):
        weight = weight + jnp.where(ids_t[k : k + 1, :] == expert_of, prob_t[k : k + 1, :], 0.0)
    place = jnp.where(weight > 0.0, mm(onehot(weight > 0.0), before, ((1,), (0,))), -1.0)
    pick = onehot(place == r_of.astype(F32))
    rest_of = jnp.where(jnp.logical_and(r_of >= CAP, r_of < PAD - 1), (r_of - CAP) * 4, -8)
    by_token = jnp.where(r_of == PAD - 1, weight, 0.0).astype(BF16)
    for b in range(4):
        cols = slice(b * 256, (b + 1) * 256)
        packed = mm(pick, payload[:, cols], ((1,), (0,)))
        packed = packed + mm(onehot(place == (rest_of + b).astype(F32)), payload[:, OUT_W:], ((1,), (0,)))
        if b == 0:
            widen = onehot(iota((TOK, 256), 0) == iota((TOK, 256), 1))
            packed = packed + mm(by_token, widen, ((1,), (0,)))
        send[:, cols] = packed.astype(BF16)
    recv[0:PAD, :] = send[0:PAD, :]

    pl.semaphore_wait(barrier, NE - 1 + 4)

    def at16(ref, rel):
        return ref.at[pl.ds(pl.multiple_of(rel * PAD, PAD), PAD), :]

    def out_copy(rel):
        return pltpu.make_async_remote_copy(
            src_ref=at16(send, rel), dst_ref=at16(recv, rel), send_sem=a_s.at[rel], recv_sem=a_r.at[rel],
            device_id=(ahead(rel), te), device_id_type=MESH,
        )

    def pass_copy(dy):
        rel = dy * NZ + NZ // 2
        return pltpu.make_async_remote_copy(
            src_ref=at16(send, rel), dst_ref=passing.at[dy - RELAYED[0]],
            send_sem=a_s.at[rel], recv_sem=p_r.at[dy - RELAYED[0]],
            device_id=(ahead(dy * NZ + WAY), te), device_id_type=MESH,
        )

    def pass_on_copy(dy):
        rel = dy * NZ + NZ // 2
        return pltpu.make_async_remote_copy(
            src_ref=passing.at[dy - RELAYED[0]], dst_ref=at16(recv, rel),
            send_sem=p_s.at[dy - RELAYED[0]], recv_sem=a_r.at[rel],
            device_id=(ahead(WAY), te), device_id_type=MESH,
        )

    def back_copy(rel):
        return pltpu.make_async_remote_copy(
            src_ref=at16(back_send, rel), dst_ref=at16(back_recv, rel), send_sem=b_s.at[rel], recv_sem=b_r.at[rel],
            device_id=(behind(rel), te), device_id_type=MESH,
        )

    def cols_of(t):
        return pl.ds(pl.multiple_of(t * WL, BLOCK), WL)

    def window(c, t, first=0, count=CH):
        return rows.at[:, pl.ds(pl.multiple_of(c * CH + first, 16), count), cols_of(t)]

    def own_rows(c):
        return own.at[:, pl.ds(pl.multiple_of(c * CH, 16), CH), :]

    def own_copy(c):
        return pltpu.make_async_copy(own_rows(c), window(c, te), sem_own.at[c])

    def gather_copy(c, k):
        ref, peer = (
            (lambda: window(c, te), t_plus),
            (lambda: window(c, te), t_minus),
            (lambda: window(c, te), t_core),
            (lambda: window(c, t_minus, 0, HALF), t_plus),
            (lambda: window(c, t_plus, HALF, HALF), t_minus),
            (lambda: window(c, t_minus), t_core),
            (lambda: window(c, t_plus), t_core),
            (lambda: window(c, t_far), t_core),
        )[k]
        ref = ref()
        return pltpu.make_async_remote_copy(
            src_ref=own_rows(c) if k < 3 else ref, dst_ref=ref, send_sem=g_s.at[k, c], recv_sem=g_r.at[k, c],
            device_id=(er, peer), device_id_type=MESH,
        )

    to_core = (x_far * 2 + other, x_plus * 2 + other, x_minus * 2 + other, t_core)

    def sum_copy(c, k):
        if k < 4:
            src, dst, peer = parts.at[k, c], core_in.at[k, c], t_core
        elif k == 4:
            src, dst, peer = far_sum.at[c, pl.ds(0, HALF), :], relay_a.at[c], t_plus
        elif k == 5:
            src, dst, peer = far_sum.at[c, pl.ds(HALF, HALF), :], relay_b.at[c], t_minus
        elif k == 6:
            src, dst, peer = plus_sum.at[c], from_minus.at[c], t_plus
        elif k == 7:
            src, dst, peer = minus_sum.at[c], from_plus.at[c], t_minus
        elif k == 8:
            src, dst, peer = gate_own.at[c], gate_core.at[c], t_core
        else:
            src, dst, peer = gate_chip.at[c], gate_in.at[k - 9, c], (t_plus, t_minus, t_far)[k - 9]
        return pltpu.make_async_remote_copy(
            src_ref=src, dst_ref=dst, send_sem=r_s.at[k, c], recv_sem=r_r.at[k, c],
            device_id=(er, peer), device_id_type=MESH,
        )

    def scales_stage():
        load_in.wait()
        load_down.wait()

        flip = onehot(iota((WIDTH // BLOCK, WIDTH // BLOCK), 0) == iota((WIDTH // BLOCK, WIDTH // BLOCK), 1))
        for part in range(3):
            left = in_scale[part * 40 : (part + 1) * 40, :] if part < 2 else down_scale[...]
            total = jnp.zeros((HID, WIDTH // BLOCK), F32)
            for _ in range(3):
                piece = left.astype(BF16)
                total = total + mm(piece, flip, ((0,), (0,)))
                left = left - piece.astype(F32)
            scales[part * HID : (part + 1) * HID, :] = total

    def scale_stage(c):
        @pl.loop(c * STEPS, (c + 1) * STEPS)
        def _(i):
            at = pl.ds(pl.multiple_of(i * 16, 16), 16)
            scale = scales[at, :]
            for q in range(WIDTH // BLOCK):
                cols = slice(q * BLOCK, (q + 1) * BLOCK)
                weights[at, cols] = (weights[at, cols].astype(F32) * scale[:, q : q + 1]).astype(BF16)

    def prepare_stage():
        ids_col = mm(eye, ids_t[...].astype(F32).astype(BF16), ((1,), (1,))).astype(jnp.int32)
        left = prob_t[...]
        prob_by_token = jnp.zeros((TOK, TOP), F32)
        for _ in range(3):
            piece = left.astype(BF16)
            prob_by_token = prob_by_token + mm(eye, piece, ((1,), (1,)))
            left = left - piece.astype(F32)
        wide = iota((TOK, NE * PAD), 1)
        wide_rel = wide >> 4
        wide_r = wide & 15
        wide_expert = ((y + (wide_rel >> 3)) & 3) * NZ + ((z + (wide_rel & 7)) & 7)
        weight = jnp.zeros((TOK, NE * PAD), F32)
        for k in range(TOP):
            weight = weight + jnp.where(ids_col[:, k : k + 1] == wide_expert, prob_by_token[:, k : k + 1], 0.0)
        earlier = onehot(iota((TOK, TOK), 1) < iota((TOK, TOK), 0))
        place = jnp.where(weight > 0.0, mm(earlier, onehot(weight > 0.0), ((1,), (0,))), -1.0)
        rest = jnp.where(jnp.logical_and(wide_r >= CAP, wide_r < PAD - 1), (wide_r - CAP) * 4, -8)
        for b in range(5):
            here = wide_r if b == 4 else rest + b
            kept = jnp.where(place == here.astype(F32), weight, 0.0)
            high = kept.astype(BF16)
            chosen[b, 0:TOK, :] = high
            chosen[b, TOK:, :] = (kept - high.astype(F32)).astype(BF16)
        lane = iota((TOK, 128), 1)
        for k in range(TOP):
            expert = ids_col[:, k : k + 1]
            rel = (((expert >> 3) - y) & 3) * NZ + (((expert & 7) - z) & 7)
            row = wide == rel * PAD + PAD - 1
            gate_pick[k * TOK : (k + 1) * TOK, :] = onehot(row)
            position = jnp.sum(jnp.where(row, place, 0.0), axis=1, keepdims=True)
            spot = ((rel & 7) * CAP).astype(F32) + position
            gate_spot[k * TOK : (k + 1) * TOK, :] = onehot(lane.astype(F32) == spot)

    def send_stage(c):
        @pl.loop(0, NZ)
        def _(i):
            rel = c * NZ + i
            relayed = jnp.logical_and(rel >= RELAYED[0] * NZ, i == NZ // 2)

            @pl.when(jnp.logical_and(rel > 0, jnp.logical_not(relayed)))
            def _():
                out_copy(rel).start()

        for dy in RELAYED:

            @pl.when(c == dy - 1)
            def _():
                pass_copy(dy).start()

    def sent_stage(c):
        @pl.loop(0, NZ)
        def _(i):
            rel = c * NZ + i
            relayed = jnp.logical_and(rel >= RELAYED[0] * NZ, i == NZ // 2)

            @pl.when(jnp.logical_and(rel > 0, jnp.logical_not(relayed)))
            def _():
                out_copy(rel).wait_send()

    send_stage(0)

    def dispatch_stage(c):
        sent_stage(c)

        @pl.when(c < NY - 1)
        def _():
            send_stage(c + 1)

        @pl.loop(0, NZ)
        def _(i):
            rel = c * NZ + i

            @pl.when(rel > 0)
            def _():
                out_copy(rel).wait_recv()

        row = iota((CH, CHP), 0)
        col = iota((CH, CHP), 1)
        group = lax.div(row, CAP)
        within = row - group * CAP
        squeeze = onehot(col == group * PAD + within)
        span = pl.ds(pl.multiple_of(c * CH, 16), CH)
        part = pl.ds(pl.multiple_of(c * CHP, CHP), CHP)
        own[0, span, :] = mm(squeeze, recv[part, :WL], ((1,), (0,))).astype(BF16)
        own[1, span, 0 : OUT_W - WL] = mm(squeeze, recv[part, WL:OUT_W], ((1,), (0,))).astype(BF16)
        rest = jnp.zeros((CH, 256), F32)
        for b in range(4):
            here = jnp.logical_and(col == group * PAD + CAP + (within >> 2), (within & 3) == b)
            rest = rest + mm(onehot(here), recv[part, b * 256 : (b + 1) * 256], ((1,), (0,)))
        own[1, span, OUT_W - WL :] = rest.astype(BF16)
        own_copy(c).start()
        for k in (0, 1, 2):
            gather_copy(c, k).start()
        named = mm(onehot(col == group * PAD + PAD - 1), recv[part, :BLOCK], ((1,), (0,)))[:, :TOK]
        rank = mm(onehot(named > 0.0), before, ((1,), (0,)))
        taken = jnp.logical_and(named > 0.0, rank == within[:, :TOK].astype(F32))
        prob_col[span, :] = jnp.sum(jnp.where(taken, named, 0.0), axis=1, keepdims=True)

        for dy in RELAYED:

            @pl.when(c == dy - 1)
            def _():
                pass_copy(dy).wait_recv()
                pass_on_copy(dy).start()

        @pl.when(c == 0)
        def _():
            scales_stage()

        scale_stage(c)

    def relay_stage(c):
        gather_copy(c, 0).wait_recv()
        gather_copy(c, 3).start()
        gather_copy(c, 5).start()
        gather_copy(c, 1).wait_recv()
        gather_copy(c, 4).start()
        gather_copy(c, 6).start()

    def far_stage(c):
        gather_copy(c, 3).wait_recv()
        gather_copy(c, 4).wait_recv()
        gather_copy(c, 7).start()

    def compute_stage(c):
        for k in (2, 5, 6, 7):
            gather_copy(c, k).wait_recv()
        own_copy(c).wait()
        span = pl.ds(pl.multiple_of(c * CH, 16), CH)
        row_values = rows[0, span, :]
        gate = mm(row_values, weights[0:HID, :], ((1,), (1,)))
        up = mm(row_values, weights[HID : 2 * HID, :], ((1,), (1,)))
        hidden = mm(rows[1, span, :], weights[2 * HID :, :], ((1,), (1,)))
        sig = jax.nn.sigmoid(gate)
        act = gate * sig
        gate_full = hidden * up * sig * (1.0 + gate * (1.0 - sig))
        up_full = hidden * act
        gate_grad = gate_full.astype(BF16)
        up_grad = up_full.astype(BF16)
        acted = act * up
        for k in range(8):
            t = (to_core + (t_far, t_plus, t_minus, te))[k]
            part = mm(gate_grad, weights[0:HID, cols_of(t)], ((1,), (0,)))
            part = part + mm(up_grad, weights[HID : 2 * HID, cols_of(t)], ((1,), (0,)))
            if k < 4:
                parts[k, c] = part.astype(BF16)
                sum_copy(c, k).start()
            else:
                kept_parts[k - 4, c] = part.astype(BF16)
        share = hidden * acted
        ones = jnp.ones((8, HID), BF16)
        gate_row = jnp.zeros((8, CH), F32)
        for _ in range(3):
            piece = share.astype(BF16)
            gate_row = gate_row + mm(ones, piece, ((1,), (1,)))
            share = share - piece.astype(F32)
        gate_own[c] = jnp.concatenate([gate_row, jnp.zeros((8, 128 - CH), F32)], axis=1)
        sum_copy(c, 8).start()
        prob = prob_col[span, :]
        hid[0, span, :] = (prob * gate_full).astype(BF16)
        hid[1, span, :] = (prob * up_full).astype(BF16)
        hid[2, span, :] = (prob * acted).astype(BF16)

    def chip_sum(c, k):
        return kept_parts[k, c].astype(F32) + core_in[k, c].astype(F32)

    def core_stage(c):
        sum_copy(c, 0).wait_recv()
        far_sum[c] = chip_sum(c, 0).astype(BF16)
        sum_copy(c, 4).start()
        sum_copy(c, 5).start()
        sum_copy(c, 8).wait_recv()
        gate_chip[c] = gate_own[c] + gate_core[c]
        for k in (9, 10, 11):
            sum_copy(c, k).start()

    def ring_stage(c):
        sum_copy(c, 1).wait_recv()
        total = chip_sum(c, 1)
        sum_copy(c, 4).wait_recv()
        plus_sum[c, 0:HALF, :] = (total[0:HALF] + relay_a[c].astype(F32)).astype(BF16)
        plus_sum[c, HALF:CH, :] = total[HALF:CH].astype(BF16)
        sum_copy(c, 6).start()
        sum_copy(c, 2).wait_recv()
        total = chip_sum(c, 2)
        sum_copy(c, 5).wait_recv()
        minus_sum[c, 0:HALF, :] = total[0:HALF].astype(BF16)
        minus_sum[c, HALF:CH, :] = (total[HALF:CH] + relay_b[c].astype(F32)).astype(BF16)
        sum_copy(c, 7).start()

    def return_stage(c):
        sum_copy(c, 3).wait_recv()
        total = chip_sum(c, 3)
        sum_copy(c, 6).wait_recv()
        sum_copy(c, 7).wait_recv()
        for k in (9, 10, 11):
            sum_copy(c, k).wait_recv()
        gate_row = (gate_chip[c] + gate_in[2, c]) + (gate_in[0, c] + gate_in[1, c])
        total = total + from_minus[c].astype(F32) + from_plus[c].astype(F32)
        row = iota((CHP, CH), 0)
        col = iota((CHP, CH), 1)
        r = row & 15
        first = (row >> 4) * CAP
        spread = onehot(jnp.logical_and(r < CAP, col == first + r))
        extra = jnp.logical_and(r >= CAP, r < PAD - 1)
        values = total.astype(BF16)
        at = pl.ds(pl.multiple_of(c * CHP, CHP), CHP)
        for b in range(4):
            out = mm(spread, values[:, b * 128 : (b + 1) * 128], ((1,), (0,)))
            there = onehot(jnp.logical_and(extra, col == first + (r - CAP) * 4 + b))
            out = out + mm(there, values[:, BACK_W:], ((1,), (0,)))
            if b == 0:
                out = out + jnp.where(iota((CHP, 128), 0) & 15 == PAD - 1, gate_row[0:1, :], 0.0)
            back_send[at, b * 128 : (b + 1) * 128] = out.astype(BF16)

        @pl.loop(0, NZ)
        def _(i):
            rel = c * NZ + i

            @pl.when(rel > 0)
            def _():
                back_copy(rel).start()

    stages = (
        (dispatch_stage, 0), (relay_stage, 1), (far_stage, 2), (compute_stage, 3),
        (core_stage, 4), (ring_stage, 5), (return_stage, 6),
    )

    @pl.loop(0, NY + 6)
    def _(s):
        for stage, lag in stages:

            @pl.when(jnp.logical_and(s >= lag, s < NY + lag))
            def _():
                stage(s - lag)

        @pl.when(s == NY)
        def _():
            prepare_stage()

        for k in range(3):

            @pl.when(s == NY + 2 + k)
            def _():
                turned = hid[k].T
                for i in range(WIDTH // STEP):
                    cols = slice(i * STEP, (i + 1) * STEP)
                    grads[k, :, cols] = mm(turned, rows[k // 2, :, cols], ((1,), (0,))).astype(BF16)

    back_recv[0:PAD, :] = back_send[0:PAD, :]
    @pl.loop(1, NE)
    def _(rel):
        back_copy(rel).wait_recv()

    total = mm(chosen[4], back_recv[...], ((1,), (0,)))
    gi_out[:, 0:BACK_W] = (total[0:TOK] + total[TOK:]).astype(BF16)
    total = jnp.zeros((2 * TOK, 128), F32)
    for b in range(4):
        total = total + mm(chosen[b], back_recv[:, b * 128 : (b + 1) * 128], ((1,), (0,)))
    gi_out[:, BACK_W:] = (total[0:TOK] + total[TOK:]).astype(BF16)
    line = mm(gate_pick[...], back_recv[:, 0:128], ((1,), (0,)))
    line = (line * gate_spot[...].astype(F32)).astype(BF16)
    line = mm(jnp.ones((TOP, 128), BF16), line, ((1,), (1,)))
    at_k = iota((TOP, TOP * TOK), 1) >> 5 == iota((TOP, TOP * TOK), 0)
    at_t = iota((TOP * TOK, TOK), 0) & 31 == iota((TOP * TOK, TOK), 1)
    gg_out[...] = mm(jnp.where(at_k, line, 0.0).astype(BF16), onehot(at_t), ((1,), (0,))).astype(BF16)

    @pl.loop(1, NE)
    def _(rel):
        back_copy(rel).wait_send()

    for dy in RELAYED:
        pass_copy(dy).wait_send()
        pass_on_copy(dy).wait_send()

    @pl.loop(0, NY)
    def _(c):
        for k in range(8):
            gather_copy(c, k).wait_send()
        for k in range(12):
            sum_copy(c, k).wait_send()


def put_grads(grads, grad_in, grad_down, sems):
    copies = [
        pltpu.make_async_copy(
            grads.at[k, pl.ds(i * PART, PART), :],
            (grad_down.at[0] if k == 2 else grad_in.at[0, k]).at[pl.ds(i * PART, PART), :],
            sems.at[k, i],
        )
        for k in range(3)
        for i in range(HID // PART)
    ]
    for copy in copies:
        copy.start()
    for copy in copies:
        copy.wait()


def on_device(
    token_codes, token_scale, grad_out, expert_ids, gate_probs, w_in, w_in_scale, w_down, w_down_scale
):
    vmem = pl.BlockSpec(memory_space=pltpu.VMEM)
    hbm = pl.BlockSpec(memory_space=pl.ANY)
    dma = pltpu.SemaphoreType.DMA
    grad_input, grad_gates, _, grads = pl.pallas_call(
        exchange,
        out_shape=(
            jax.ShapeDtypeStruct((TOK, WL), BF16),
            jax.ShapeDtypeStruct((TOP, TOK), BF16),
            pltpu.VMEM((2, ROWS, WIDTH), BF16),
            pltpu.VMEM((3, HID, WIDTH), BF16),
        ),
        in_specs=[vmem] * 7 + [hbm] * 2,
        out_specs=(vmem, vmem, vmem, vmem),
        scratch_shapes=[
            pltpu.VMEM((TOK, 2 * WL), BF16),
            pltpu.VMEM((3 * HID, WIDTH // BLOCK), F32),
            pltpu.VMEM((NE * PAD, OUT_W), BF16),
            pltpu.VMEM((NE * PAD, OUT_W), BF16),
            pltpu.VMEM((len(RELAYED), PAD, OUT_W), BF16),
            pltpu.VMEM((2, ROWS, WL), BF16),
            pltpu.VMEM((3 * HID, WIDTH), BF16),
            pltpu.VMEM((4, NY, CH, WL), BF16),
            pltpu.VMEM((4, NY, CH, WL), BF16),
            pltpu.VMEM((4, NY, CH, WL), BF16),
            pltpu.VMEM((NY, 8, 128), F32),
            pltpu.VMEM((NY, 8, 128), F32),
            pltpu.VMEM((NY, 8, 128), F32),
            pltpu.VMEM((3, NY, 8, 128), F32),
            pltpu.VMEM((3, ROWS, HID), BF16),
            pltpu.VMEM((NY, CH, WL), BF16),
            pltpu.VMEM((NY, CH, WL), BF16),
            pltpu.VMEM((NY, CH, WL), BF16),
            pltpu.VMEM((NY, HALF, WL), BF16),
            pltpu.VMEM((NY, HALF, WL), BF16),
            pltpu.VMEM((NY, CH, WL), BF16),
            pltpu.VMEM((NY, CH, WL), BF16),
            pltpu.VMEM((NE * PAD, BACK_W), BF16),
            pltpu.VMEM((NE * PAD, BACK_W), BF16),
            pltpu.VMEM((5, 2 * TOK, NE * PAD), BF16),
            pltpu.VMEM((TOP * TOK, NE * PAD), BF16),
            pltpu.VMEM((TOP * TOK, 128), BF16),
            pltpu.VMEM((ROWS, 1), F32),
            dma((2,)),
            dma((NY,)),
            dma((NE,)),
            dma((NE,)),
            dma((len(RELAYED),)),
            dma((len(RELAYED),)),
            dma((8, NY)),
            dma((8, NY)),
            dma((12, NY)),
            dma((12, NY)),
            dma((NE,)),
            dma((NE,)),
        ],
        compiler_params=pltpu.CompilerParams(
            collective_id=0, has_side_effects=True, vmem_limit_bytes=44 * 1024 * 1024
        ),
    )(
        expert_ids.T, gate_probs.T, token_codes, token_scale.T, grad_out,
        w_in_scale.transpose(0, 1, 3, 2).reshape(2 * (WIDTH // BLOCK), HID),
        w_down_scale.transpose(0, 2, 1).reshape(WIDTH // BLOCK, HID),
        w_in.reshape(2 * HID, WIDTH), w_down.reshape(HID, WIDTH),
    )
    grad_w_in, grad_w_down = pl.pallas_call(
        put_grads,
        in_specs=[vmem],
        out_specs=(hbm, hbm),
        out_shape=(
            jax.ShapeDtypeStruct((1, 2, HID, WIDTH), BF16),
            jax.ShapeDtypeStruct((1, HID, WIDTH), BF16),
        ),
        scratch_shapes=[dma((3, HID // PART))],
        compiler_params=pltpu.CompilerParams(vmem_limit_bytes=8 * 1024 * 1024),
    )(grads)
    return (grad_input, grad_gates.T, grad_w_in, grad_w_down)


def solution(mesh):
    placed = (
        P("expert", "tensor"),
        P("expert", "tensor"),
        P("expert", "tensor"),
        P("expert", None),
        P("expert", None),
        P("expert", None, "tensor", None),
        P("expert", None, "tensor", None),
        P("expert", "tensor", None),
        P("expert", "tensor", None),
    )
    return jax.shard_map(
        on_device,
        mesh=mesh,
        in_specs=placed,
        out_specs=(
            P("expert", "tensor"),
            P("expert", None),
            P("expert", None, "tensor", None),
            P("expert", "tensor", None),
        ),
        check_vma=False,
    )
```

```python
import functools

import jax
import jax.numpy as jnp
from jax import lax
from jax.experimental import pallas as pl
from jax.experimental.pallas import tpu as pltpu
from jax.sharding import PartitionSpec as P

MESH = pl.DeviceIdType.MESH
BLOCK = 128
CAP = 12
PAD = 16
NX, NY, NZ = 4, 4, 8
NE = NY * NZ
TOK = 32
TOP = 8
WL = 640
WIDTH = 5120
HID = 192
ROWS = NE * CAP
CH = NZ * CAP
CHP = NZ * PAD
HALF = CH // 2
OUT_W = 4 * 256
BACK_W = 4 * 128
RELAYED = (2, 3)
WAY = NZ - 2
STEP = 512
PART = 48
STEPS = 3 * HID // 16 // NY
F32 = jnp.float32
BF16 = jnp.bfloat16


def mm(a, b, dims):
    return lax.dot_general(a, b, (dims, ((), ())), preferred_element_type=F32)


def iota(shape, axis):
    return lax.broadcasted_iota(jnp.int32, shape, axis)


def onehot(mask):
    return jnp.where(mask, 1.0, 0.0).astype(BF16)


def exchange(
    ids_hbm, prob_hbm, codes_hbm, tok_scale_hbm, grad_hbm, in_scale_hbm, down_scale_hbm, w_in, w_down,
    gi_out, gg_out, grads, rows,
    ids_t, prob_t, codes, tok_scale, grad_out, in_scale, down_scale,
    payload, scales, send, recv, passing, own, weights, parts, kept_parts, core_in, gate_own, gate_core, gate_chip, gate_in, hid, far_sum, plus_sum, minus_sum,
    relay_a, relay_b, from_minus, from_plus, back_send, back_recv, chosen, gate_pick, gate_spot, prob_col,
    sem_in, sem_w, sem_own, a_s, a_r, p_s, p_r, g_s, g_r, r_s, r_r, b_s, b_r,
):
    er = lax.axis_index("expert")
    te = lax.axis_index("tensor")
    y, z = lax.div(er, NZ), lax.rem(er, NZ)
    x, core = lax.div(te, 2), lax.rem(te, 2)
    other = 1 - core
    x_plus, x_minus, x_far = lax.rem(x + 1, NX), lax.rem(x + 3, NX), lax.rem(x + 2, NX)
    t_plus, t_minus, t_far = x_plus * 2 + core, x_minus * 2 + core, x_far * 2 + core
    t_core = x * 2 + other

    def ahead(rel):
        dy, dz = lax.div(rel, NZ), lax.rem(rel, NZ)
        return lax.rem(y + dy, NY) * NZ + lax.rem(z + dz, NZ)

    def behind(rel):
        dy, dz = lax.div(rel, NZ), lax.rem(rel, NZ)
        return lax.rem(y + NY - dy, NY) * NZ + lax.rem(z + NZ - dz, NZ)

    barrier = pltpu.get_barrier_semaphore()

    @pl.loop(1, NE)
    def _(rel):
        pl.semaphore_signal(barrier, inc=1, device_id=(ahead(rel), te), device_id_type=MESH)

    for peer in (t_plus, t_minus, t_core, t_far):
        pl.semaphore_signal(barrier, inc=1, device_id=(er, peer), device_id_type=MESH)

    loads = [
        pltpu.make_async_copy(src, dst, sem_in.at[i])
        for i, (src, dst) in enumerate(
            (
                (ids_hbm, ids_t), (prob_hbm, prob_t), (codes_hbm, codes), (tok_scale_hbm, tok_scale),
                (grad_hbm, grad_out), (in_scale_hbm, in_scale), (down_scale_hbm, down_scale),
            )
        )
    ]
    for load in loads:
        load.start()
    load_in = pltpu.make_async_copy(w_in, weights.at[pl.ds(0, 2 * HID), :], sem_w.at[0])
    load_down = pltpu.make_async_copy(w_down, weights.at[pl.ds(2 * HID, HID), :], sem_w.at[1])
    load_in.start()
    load_down.start()
    for load in loads[:5]:
        load.wait()

    eye = onehot(iota((TOK, TOK), 0) == iota((TOK, TOK), 1))
    before = onehot(iota((TOK, TOK), 0) < iota((TOK, TOK), 1))
    tok_cols = mm(eye, tok_scale[...], ((1,), (1,)))
    for j in range(WL // BLOCK):
        cols = slice(j * BLOCK, (j + 1) * BLOCK)
        payload[:, cols] = (codes[:, cols].astype(F32) * tok_cols[:, j : j + 1]).astype(BF16)
    payload[:, WL:] = grad_out[...]

    slot = iota((NE * PAD, TOK), 0)
    rel_of = slot >> 4
    r_of = slot & 15
    expert_of = ((y + (rel_of >> 3)) & 3) * NZ + ((z + (rel_of & 7)) & 7)
    weight = jnp.zeros((NE * PAD, TOK), F32)
    for k in range(TOP):
        weight = weight + jnp.where(ids_t[k : k + 1, :] == expert_of, prob_t[k : k + 1, :], 0.0)
    place = jnp.where(weight > 0.0, mm(onehot(weight > 0.0), before, ((1,), (0,))), -1.0)
    pick = onehot(place == r_of.astype(F32))
    rest_of = jnp.where(jnp.logical_and(r_of >= CAP, r_of < PAD - 1), (r_of - CAP) * 4, -8)
    by_token = jnp.where(r_of == PAD - 1, weight, 0.0).astype(BF16)
    for b in range(4):
        cols = slice(b * 256, (b + 1) * 256)
        packed = mm(pick, payload[:, cols], ((1,), (0,)))
        packed = packed + mm(onehot(place == (rest_of + b).astype(F32)), payload[:, OUT_W:], ((1,), (0,)))
        if b == 0:
            widen = onehot(iota((TOK, 256), 0) == iota((TOK, 256), 1))
            packed = packed + mm(by_token, widen, ((1,), (0,)))
        send[:, cols] = packed.astype(BF16)
    recv[0:PAD, :] = send[0:PAD, :]

    pl.semaphore_wait(barrier, NE - 1 + 4)

    def at16(ref, rel):
        return ref.at[pl.ds(pl.multiple_of(rel * PAD, PAD), PAD), :]

    def out_copy(rel):
        return pltpu.make_async_remote_copy(
            src_ref=at16(send, rel), dst_ref=at16(recv, rel), send_sem=a_s.at[rel], recv_sem=a_r.at[rel],
            device_id=(ahead(rel), te), device_id_type=MESH,
        )

    def pass_copy(dy):
        rel = dy * NZ + NZ // 2
        return pltpu.make_async_remote_copy(
            src_ref=at16(send, rel), dst_ref=passing.at[dy - RELAYED[0]],
            send_sem=a_s.at[rel], recv_sem=p_r.at[dy - RELAYED[0]],
            device_id=(ahead(dy * NZ + WAY), te), device_id_type=MESH,
        )

    def pass_on_copy(dy):
        rel = dy * NZ + NZ // 2
        return pltpu.make_async_remote_copy(
            src_ref=passing.at[dy - RELAYED[0]], dst_ref=at16(recv, rel),
            send_sem=p_s.at[dy - RELAYED[0]], recv_sem=a_r.at[rel],
            device_id=(ahead(WAY), te), device_id_type=MESH,
        )

    def back_copy(rel):
        return pltpu.make_async_remote_copy(
            src_ref=at16(back_send, rel), dst_ref=at16(back_recv, rel), send_sem=b_s.at[rel], recv_sem=b_r.at[rel],
            device_id=(behind(rel), te), device_id_type=MESH,
        )

    def cols_of(t):
        return pl.ds(pl.multiple_of(t * WL, BLOCK), WL)

    def window(c, t, first=0, count=CH):
        return rows.at[:, pl.ds(pl.multiple_of(c * CH + first, 16), count), cols_of(t)]

    def own_rows(c):
        return own.at[:, pl.ds(pl.multiple_of(c * CH, 16), CH), :]

    def own_copy(c):
        return pltpu.make_async_copy(own_rows(c), window(c, te), sem_own.at[c])

    def gather_copy(c, k):
        ref, peer = (
            (lambda: window(c, te), t_plus),
            (lambda: window(c, te), t_minus),
            (lambda: window(c, te), t_core),
            (lambda: window(c, t_minus, 0, HALF), t_plus),
            (lambda: window(c, t_plus, HALF, HALF), t_minus),
            (lambda: window(c, t_minus), t_core),
            (lambda: window(c, t_plus), t_core),
            (lambda: window(c, t_far), t_core),
        )[k]
        ref = ref()
        return pltpu.make_async_remote_copy(
            src_ref=own_rows(c) if k < 3 else ref, dst_ref=ref, send_sem=g_s.at[k, c], recv_sem=g_r.at[k, c],
            device_id=(er, peer), device_id_type=MESH,
        )

    to_core = (x_far * 2 + other, x_plus * 2 + other, x_minus * 2 + other, t_core)

    def sum_copy(c, k):
        if k < 4:
            src, dst, peer = parts.at[k, c], core_in.at[k, c], t_core
        elif k == 4:
            src, dst, peer = far_sum.at[c, pl.ds(0, HALF), :], relay_a.at[c], t_plus
        elif k == 5:
            src, dst, peer = far_sum.at[c, pl.ds(HALF, HALF), :], relay_b.at[c], t_minus
        elif k == 6:
            src, dst, peer = plus_sum.at[c], from_minus.at[c], t_plus
        elif k == 7:
            src, dst, peer = minus_sum.at[c], from_plus.at[c], t_minus
        elif k == 8:
            src, dst, peer = gate_own.at[c], gate_core.at[c], t_core
        else:
            src, dst, peer = gate_chip.at[c], gate_in.at[k - 9, c], (t_plus, t_minus, t_far)[k - 9]
        return pltpu.make_async_remote_copy(
            src_ref=src, dst_ref=dst, send_sem=r_s.at[k, c], recv_sem=r_r.at[k, c],
            device_id=(er, peer), device_id_type=MESH,
        )

    def scales_stage():
        for load in loads[5:]:
            load.wait()
        load_in.wait()
        load_down.wait()

        flip = onehot(iota((WIDTH // BLOCK, WIDTH // BLOCK), 0) == iota((WIDTH // BLOCK, WIDTH // BLOCK), 1))
        for part in range(3):
            left = in_scale[part * 40 : (part + 1) * 40, :] if part < 2 else down_scale[...]
            total = jnp.zeros((HID, WIDTH // BLOCK), F32)
            for _ in range(3):
                piece = left.astype(BF16)
                total = total + mm(piece, flip, ((0,), (0,)))
                left = left - piece.astype(F32)
            scales[part * HID : (part + 1) * HID, :] = total

    def scale_stage(c):
        @pl.loop(c * STEPS, (c + 1) * STEPS)
        def _(i):
            at = pl.ds(pl.multiple_of(i * 16, 16), 16)
            scale = scales[at, :]
            for q in range(WIDTH // BLOCK):
                cols = slice(q * BLOCK, (q + 1) * BLOCK)
                weights[at, cols] = (weights[at, cols].astype(F32) * scale[:, q : q + 1]).astype(BF16)

    def prepare_stage():
        ids_col = mm(eye, ids_t[...].astype(F32).astype(BF16), ((1,), (1,))).astype(jnp.int32)
        left = prob_t[...]
        prob_by_token = jnp.zeros((TOK, TOP), F32)
        for _ in range(3):
            piece = left.astype(BF16)
            prob_by_token = prob_by_token + mm(eye, piece, ((1,), (1,)))
            left = left - piece.astype(F32)
        wide = iota((TOK, NE * PAD), 1)
        wide_rel = wide >> 4
        wide_r = wide & 15
        wide_expert = ((y + (wide_rel >> 3)) & 3) * NZ + ((z + (wide_rel & 7)) & 7)
        weight = jnp.zeros((TOK, NE * PAD), F32)
        for k in range(TOP):
            weight = weight + jnp.where(ids_col[:, k : k + 1] == wide_expert, prob_by_token[:, k : k + 1], 0.0)
        earlier = onehot(iota((TOK, TOK), 1) < iota((TOK, TOK), 0))
        place = jnp.where(weight > 0.0, mm(earlier, onehot(weight > 0.0), ((1,), (0,))), -1.0)
        rest = jnp.where(jnp.logical_and(wide_r >= CAP, wide_r < PAD - 1), (wide_r - CAP) * 4, -8)
        for b in range(5):
            here = wide_r if b == 4 else rest + b
            kept = jnp.where(place == here.astype(F32), weight, 0.0)
            high = kept.astype(BF16)
            chosen[b, 0:TOK, :] = high
            chosen[b, TOK:, :] = (kept - high.astype(F32)).astype(BF16)
        lane = iota((TOK, 128), 1)
        for k in range(TOP):
            expert = ids_col[:, k : k + 1]
            rel = (((expert >> 3) - y) & 3) * NZ + (((expert & 7) - z) & 7)
            row = wide == rel * PAD + PAD - 1
            gate_pick[k * TOK : (k + 1) * TOK, :] = onehot(row)
            position = jnp.sum(jnp.where(row, place, 0.0), axis=1, keepdims=True)
            spot = ((rel & 7) * CAP).astype(F32) + position
            gate_spot[k * TOK : (k + 1) * TOK, :] = onehot(lane.astype(F32) == spot)

    def send_stage(c):
        @pl.loop(0, NZ)
        def _(i):
            rel = c * NZ + i
            relayed = jnp.logical_and(rel >= RELAYED[0] * NZ, i == NZ // 2)

            @pl.when(jnp.logical_and(rel > 0, jnp.logical_not(relayed)))
            def _():
                out_copy(rel).start()

        for dy in RELAYED:

            @pl.when(c == dy - 1)
            def _():
                pass_copy(dy).start()

    def sent_stage(c):
        @pl.loop(0, NZ)
        def _(i):
            rel = c * NZ + i
            relayed = jnp.logical_and(rel >= RELAYED[0] * NZ, i == NZ // 2)

            @pl.when(jnp.logical_and(rel > 0, jnp.logical_not(relayed)))
            def _():
                out_copy(rel).wait_send()

    send_stage(0)

    def dispatch_stage(c):
        sent_stage(c)

        @pl.when(c < NY - 1)
        def _():
            send_stage(c + 1)

        @pl.loop(0, NZ)
        def _(i):
            rel = c * NZ + i

            @pl.when(rel > 0)
            def _():
                out_copy(rel).wait_recv()

        row = iota((CH, CHP), 0)
        col = iota((CH, CHP), 1)
        group = lax.div(row, CAP)
        within = row - group * CAP
        squeeze = onehot(col == group * PAD + within)
        span = pl.ds(pl.multiple_of(c * CH, 16), CH)
        part = pl.ds(pl.multiple_of(c * CHP, CHP), CHP)
        own[0, span, :] = mm(squeeze, recv[part, :WL], ((1,), (0,))).astype(BF16)
        own[1, span, 0 : OUT_W - WL] = mm(squeeze, recv[part, WL:OUT_W], ((1,), (0,))).astype(BF16)
        rest = jnp.zeros((CH, 256), F32)
        for b in range(4):
            here = jnp.logical_and(col == group * PAD + CAP + (within >> 2), (within & 3) == b)
            rest = rest + mm(onehot(here), recv[part, b * 256 : (b + 1) * 256], ((1,), (0,)))
        own[1, span, OUT_W - WL :] = rest.astype(BF16)
        own_copy(c).start()
        for k in (0, 1, 2):
            gather_copy(c, k).start()
        named = mm(onehot(col == group * PAD + PAD - 1), recv[part, :BLOCK], ((1,), (0,)))[:, :TOK]
        rank = mm(onehot(named > 0.0), before, ((1,), (0,)))
        taken = jnp.logical_and(named > 0.0, rank == within[:, :TOK].astype(F32))
        prob_col[span, :] = jnp.sum(jnp.where(taken, named, 0.0), axis=1, keepdims=True)

        for dy in RELAYED:

            @pl.when(c == dy - 1)
            def _():
                pass_copy(dy).wait_recv()
                pass_on_copy(dy).start()

        @pl.when(c == 0)
        def _():
            scales_stage()

        scale_stage(c)

    def relay_stage(c):
        gather_copy(c, 0).wait_recv()
        gather_copy(c, 3).start()
        gather_copy(c, 5).start()
        gather_copy(c, 1).wait_recv()
        gather_copy(c, 4).start()
        gather_copy(c, 6).start()

    def far_stage(c):
        gather_copy(c, 3).wait_recv()
        gather_copy(c, 4).wait_recv()
        gather_copy(c, 7).start()

    def compute_stage(c):
        for k in (2, 5, 6, 7):
            gather_copy(c, k).wait_recv()
        own_copy(c).wait()
        span = pl.ds(pl.multiple_of(c * CH, 16), CH)
        row_values = rows[0, span, :]
        gate = mm(row_values, weights[0:HID, :], ((1,), (1,)))
        up = mm(row_values, weights[HID : 2 * HID, :], ((1,), (1,)))
        hidden = mm(rows[1, span, :], weights[2 * HID :, :], ((1,), (1,)))
        sig = jax.nn.sigmoid(gate)
        act = gate * sig
        gate_full = hidden * up * sig * (1.0 + gate * (1.0 - sig))
        up_full = hidden * act
        gate_grad = gate_full.astype(BF16)
        up_grad = up_full.astype(BF16)
        acted = act * up
        for k in range(8):
            t = (to_core + (t_far, t_plus, t_minus, te))[k]
            part = mm(gate_grad, weights[0:HID, cols_of(t)], ((1,), (0,)))
            part = part + mm(up_grad, weights[HID : 2 * HID, cols_of(t)], ((1,), (0,)))
            if k < 4:
                parts[k, c] = part.astype(BF16)
                sum_copy(c, k).start()
            else:
                kept_parts[k - 4, c] = part.astype(BF16)
        share = hidden * acted
        ones = jnp.ones((8, HID), BF16)
        gate_row = jnp.zeros((8, CH), F32)
        for _ in range(3):
            piece = share.astype(BF16)
            gate_row = gate_row + mm(ones, piece, ((1,), (1,)))
            share = share - piece.astype(F32)
        gate_own[c] = jnp.concatenate([gate_row, jnp.zeros((8, 128 - CH), F32)], axis=1)
        sum_copy(c, 8).start()
        prob = prob_col[span, :]
        hid[0, span, :] = (prob * gate_full).astype(BF16)
        hid[1, span, :] = (prob * up_full).astype(BF16)
        hid[2, span, :] = (prob * acted).astype(BF16)

    def chip_sum(c, k):
        return kept_parts[k, c].astype(F32) + core_in[k, c].astype(F32)

    def core_stage(c):
        sum_copy(c, 0).wait_recv()
        far_sum[c] = chip_sum(c, 0).astype(BF16)
        sum_copy(c, 4).start()
        sum_copy(c, 5).start()
        sum_copy(c, 8).wait_recv()
        gate_chip[c] = gate_own[c] + gate_core[c]
        for k in (9, 10, 11):
            sum_copy(c, k).start()

    def ring_stage(c):
        sum_copy(c, 1).wait_recv()
        total = chip_sum(c, 1)
        sum_copy(c, 4).wait_recv()
        plus_sum[c, 0:HALF, :] = (total[0:HALF] + relay_a[c].astype(F32)).astype(BF16)
        plus_sum[c, HALF:CH, :] = total[HALF:CH].astype(BF16)
        sum_copy(c, 6).start()
        sum_copy(c, 2).wait_recv()
        total = chip_sum(c, 2)
        sum_copy(c, 5).wait_recv()
        minus_sum[c, 0:HALF, :] = total[0:HALF].astype(BF16)
        minus_sum[c, HALF:CH, :] = (total[HALF:CH] + relay_b[c].astype(F32)).astype(BF16)
        sum_copy(c, 7).start()

    def return_stage(c):
        sum_copy(c, 3).wait_recv()
        total = chip_sum(c, 3)
        sum_copy(c, 6).wait_recv()
        sum_copy(c, 7).wait_recv()
        for k in (9, 10, 11):
            sum_copy(c, k).wait_recv()
        gate_row = (gate_chip[c] + gate_in[2, c]) + (gate_in[0, c] + gate_in[1, c])
        total = total + from_minus[c].astype(F32) + from_plus[c].astype(F32)
        row = iota((CHP, CH), 0)
        col = iota((CHP, CH), 1)
        r = row & 15
        first = (row >> 4) * CAP
        spread = onehot(jnp.logical_and(r < CAP, col == first + r))
        extra = jnp.logical_and(r >= CAP, r < PAD - 1)
        values = total.astype(BF16)
        at = pl.ds(pl.multiple_of(c * CHP, CHP), CHP)
        for b in range(4):
            out = mm(spread, values[:, b * 128 : (b + 1) * 128], ((1,), (0,)))
            there = onehot(jnp.logical_and(extra, col == first + (r - CAP) * 4 + b))
            out = out + mm(there, values[:, BACK_W:], ((1,), (0,)))
            if b == 0:
                out = out + jnp.where(iota((CHP, 128), 0) & 15 == PAD - 1, gate_row[0:1, :], 0.0)
            back_send[at, b * 128 : (b + 1) * 128] = out.astype(BF16)

        @pl.loop(0, NZ)
        def _(i):
            rel = c * NZ + i

            @pl.when(rel > 0)
            def _():
                back_copy(rel).start()

    stages = (
        (dispatch_stage, 0), (relay_stage, 1), (far_stage, 2), (compute_stage, 3),
        (core_stage, 4), (ring_stage, 5), (return_stage, 6),
    )

    @pl.loop(0, NY + 6)
    def _(s):
        for stage, lag in stages:

            @pl.when(jnp.logical_and(s >= lag, s < NY + lag))
            def _():
                stage(s - lag)

        @pl.when(s == NY)
        def _():
            prepare_stage()

        for k in range(3):

            @pl.when(s == NY + 2 + k)
            def _():
                turned = hid[k].T
                for i in range(WIDTH // STEP):
                    cols = slice(i * STEP, (i + 1) * STEP)
                    grads[k, :, cols] = mm(turned, rows[k // 2, :, cols], ((1,), (0,))).astype(BF16)

    back_recv[0:PAD, :] = back_send[0:PAD, :]
    for dy in RELAYED:
        pass_copy(dy).wait_send()
        pass_on_copy(dy).wait_send()

    @pl.loop(0, NY)
    def _(c):
        for k in range(8):
            gather_copy(c, k).wait_send()
        for k in range(12):
            sum_copy(c, k).wait_send()

    @pl.loop(1, NE)
    def _(rel):
        back_copy(rel).wait_send()
        back_copy(rel).wait_recv()

    total = mm(chosen[4], back_recv[...], ((1,), (0,)))
    gi_out[:, 0:BACK_W] = (total[0:TOK] + total[TOK:]).astype(BF16)
    total = jnp.zeros((2 * TOK, 128), F32)
    for b in range(4):
        total = total + mm(chosen[b], back_recv[:, b * 128 : (b + 1) * 128], ((1,), (0,)))
    gi_out[:, BACK_W:] = (total[0:TOK] + total[TOK:]).astype(BF16)
    line = mm(gate_pick[...], back_recv[:, 0:128], ((1,), (0,)))
    line = (line * gate_spot[...].astype(F32)).astype(BF16)
    line = mm(jnp.ones((TOP, 128), BF16), line, ((1,), (1,)))
    at_k = iota((TOP, TOP * TOK), 1) >> 5 == iota((TOP, TOP * TOK), 0)
    at_t = iota((TOP * TOK, TOK), 0) & 31 == iota((TOP * TOK, TOK), 1)
    gg_out[...] = mm(jnp.where(at_k, line, 0.0).astype(BF16), onehot(at_t), ((1,), (0,))).astype(BF16)


def put_grads(grads, gi, gg, grad_in, grad_down, gi_out, gg_out, sems, small):
    copies = [
        pltpu.make_async_copy(
            grads.at[k, pl.ds(i * PART, PART), :],
            (grad_down.at[0] if k == 2 else grad_in.at[0, k]).at[pl.ds(i * PART, PART), :],
            sems.at[k, i],
        )
        for k in range(3)
        for i in range(HID // PART)
    ]
    copies += [pltpu.make_async_copy(gi, gi_out, small.at[0]), pltpu.make_async_copy(gg, gg_out, small.at[1])]
    for copy in copies:
        copy.start()
    for copy in copies:
        copy.wait()


def on_device(
    token_codes, token_scale, grad_out, expert_ids, gate_probs, w_in, w_in_scale, w_down, w_down_scale
):
    vmem = pl.BlockSpec(memory_space=pltpu.VMEM)
    hbm = pl.BlockSpec(memory_space=pl.ANY)
    dma = pltpu.SemaphoreType.DMA
    input_sum, gate_sum, grads = pl.pallas_call(
        exchange,
        out_shape=(
            pltpu.VMEM((TOK, WL), BF16),
            pltpu.VMEM((TOP, TOK), BF16),
            pltpu.VMEM((3, HID, WIDTH), BF16),
        ),
        in_specs=[hbm] * 9,
        out_specs=(vmem, vmem, vmem),
        scratch_shapes=[
            pltpu.VMEM((2, ROWS, WIDTH), BF16),
            pltpu.VMEM((TOP, TOK), jnp.int32),
            pltpu.VMEM((TOP, TOK), F32),
            pltpu.VMEM((TOK, WL), BF16),
            pltpu.VMEM((WL // BLOCK, TOK), BF16),
            pltpu.VMEM((TOK, WL), BF16),
            pltpu.VMEM((2 * (WIDTH // BLOCK), HID), F32),
            pltpu.VMEM((WIDTH // BLOCK, HID), F32),
            pltpu.VMEM((TOK, 2 * WL), BF16),
            pltpu.VMEM((3 * HID, WIDTH // BLOCK), F32),
            pltpu.VMEM((NE * PAD, OUT_W), BF16),
            pltpu.VMEM((NE * PAD, OUT_W), BF16),
            pltpu.VMEM((len(RELAYED), PAD, OUT_W), BF16),
            pltpu.VMEM((2, ROWS, WL), BF16),
            pltpu.VMEM((3 * HID, WIDTH), BF16),
            pltpu.VMEM((4, NY, CH, WL), BF16),
            pltpu.VMEM((4, NY, CH, WL), BF16),
            pltpu.VMEM((4, NY, CH, WL), BF16),
            pltpu.VMEM((NY, 8, 128), F32),
            pltpu.VMEM((NY, 8, 128), F32),
            pltpu.VMEM((NY, 8, 128), F32),
            pltpu.VMEM((3, NY, 8, 128), F32),
            pltpu.VMEM((3, ROWS, HID), BF16),
            pltpu.VMEM((NY, CH, WL), BF16),
            pltpu.VMEM((NY, CH, WL), BF16),
            pltpu.VMEM((NY, CH, WL), BF16),
            pltpu.VMEM((NY, HALF, WL), BF16),
            pltpu.VMEM((NY, HALF, WL), BF16),
            pltpu.VMEM((NY, CH, WL), BF16),
            pltpu.VMEM((NY, CH, WL), BF16),
            pltpu.VMEM((NE * PAD, BACK_W), BF16),
            pltpu.VMEM((NE * PAD, BACK_W), BF16),
            pltpu.VMEM((5, 2 * TOK, NE * PAD), BF16),
            pltpu.VMEM((TOP * TOK, NE * PAD), BF16),
            pltpu.VMEM((TOP * TOK, 128), BF16),
            pltpu.VMEM((ROWS, 1), F32),
            dma((7,)),
            dma((2,)),
            dma((NY,)),
            dma((NE,)),
            dma((NE,)),
            dma((len(RELAYED),)),
            dma((len(RELAYED),)),
            dma((8, NY)),
            dma((8, NY)),
            dma((12, NY)),
            dma((12, NY)),
            dma((NE,)),
            dma((NE,)),
        ],
        compiler_params=pltpu.CompilerParams(
            collective_id=0, has_side_effects=True, vmem_limit_bytes=52 * 1024 * 1024
        ),
    )(
        expert_ids.T, gate_probs.T, token_codes, token_scale.T, grad_out,
        w_in_scale.transpose(0, 1, 3, 2).reshape(2 * (WIDTH // BLOCK), HID),
        w_down_scale.transpose(0, 2, 1).reshape(WIDTH // BLOCK, HID),
        w_in.reshape(2 * HID, WIDTH), w_down.reshape(HID, WIDTH),
    )
    grad_w_in, grad_w_down, grad_input, grad_gates = pl.pallas_call(
        put_grads,
        in_specs=[vmem] * 3,
        out_specs=(hbm,) * 4,
        out_shape=(
            jax.ShapeDtypeStruct((1, 2, HID, WIDTH), BF16),
            jax.ShapeDtypeStruct((1, HID, WIDTH), BF16),
            jax.ShapeDtypeStruct((TOK, WL), BF16),
            jax.ShapeDtypeStruct((TOP, TOK), BF16),
        ),
        scratch_shapes=[dma((3, HID // PART)), dma((2,))],
        compiler_params=pltpu.CompilerParams(vmem_limit_bytes=8 * 1024 * 1024),
    )(grads, input_sum, gate_sum)
    return (grad_input, grad_gates.T, grad_w_in, grad_w_down)


def solution(mesh):
    placed = (
        P("expert", "tensor"),
        P("expert", "tensor"),
        P("expert", "tensor"),
        P("expert", None),
        P("expert", None),
        P("expert", None, "tensor", None),
        P("expert", None, "tensor", None),
        P("expert", "tensor", None),
        P("expert", "tensor", None),
    )
    return jax.shard_map(
        on_device,
        mesh=mesh,
        in_specs=placed,
        out_specs=(
            P("expert", "tensor"),
            P("expert", None),
            P("expert", None, "tensor", None),
            P("expert", "tensor", None),
        ),
        check_vma=False,
    )
```

```python
import functools

import jax
import jax.numpy as jnp
from jax import lax
from jax.experimental import pallas as pl
from jax.experimental.pallas import tpu as pltpu
from jax.sharding import PartitionSpec as P

MESH = pl.DeviceIdType.MESH
BLOCK = 128
CAP = 12
PAD = 16
NX, NY, NZ = 4, 4, 8
NE = NY * NZ
TOK = 32
TOP = 8
WL = 640
WIDTH = 5120
HID = 192
ROWS = NE * CAP
CH = NZ * CAP
CHP = NZ * PAD
HALF = CH // 2
OUT_W = 4 * 256
BACK_W = 4 * 128
RELAYED = (2, 3)
WAY = NZ - 2
STEP = 512
PART = 48
STEPS = 3 * HID // 16 // NY
F32 = jnp.float32
BF16 = jnp.bfloat16


def mm(a, b, dims):
    return lax.dot_general(a, b, (dims, ((), ())), preferred_element_type=F32)


def iota(shape, axis):
    return lax.broadcasted_iota(jnp.int32, shape, axis)


def onehot(mask):
    return jnp.where(mask, 1.0, 0.0).astype(BF16)


def exchange(
    ids_hbm, prob_hbm, codes_hbm, tok_scale_hbm, grad_hbm, in_scale_hbm, down_scale_hbm, w_in, w_down,
    gi_out, gg_out, grads, rows,
    ids_t, prob_t, codes, tok_scale, grad_out, in_scale, down_scale,
    payload, scales, send, recv, passing, own, weights, parts, kept_parts, core_in, gate_own, gate_core, gate_chip, gate_in, hid, far_sum, plus_sum, minus_sum,
    relay_a, relay_b, from_minus, from_plus, back_send, back_recv, chosen, gate_pick, gate_spot, prob_col,
    sem_in, sem_w, sem_own, a_s, a_r, p_s, p_r, g_s, g_r, r_s, r_r, b_s, b_r,
):
    er = lax.axis_index("expert")
    te = lax.axis_index("tensor")
    y, z = lax.div(er, NZ), lax.rem(er, NZ)
    x, core = lax.div(te, 2), lax.rem(te, 2)
    other = 1 - core
    x_plus, x_minus, x_far = lax.rem(x + 1, NX), lax.rem(x + 3, NX), lax.rem(x + 2, NX)
    t_plus, t_minus, t_far = x_plus * 2 + core, x_minus * 2 + core, x_far * 2 + core
    t_core = x * 2 + other

    def ahead(rel):
        dy, dz = lax.div(rel, NZ), lax.rem(rel, NZ)
        return lax.rem(y + dy, NY) * NZ + lax.rem(z + dz, NZ)

    def behind(rel):
        dy, dz = lax.div(rel, NZ), lax.rem(rel, NZ)
        return lax.rem(y + NY - dy, NY) * NZ + lax.rem(z + NZ - dz, NZ)

    barrier = pltpu.get_barrier_semaphore()

    @pl.loop(1, NE)
    def _(rel):
        pl.semaphore_signal(barrier, inc=1, device_id=(ahead(rel), te), device_id_type=MESH)

    for peer in (t_plus, t_minus, t_core, t_far):
        pl.semaphore_signal(barrier, inc=1, device_id=(er, peer), device_id_type=MESH)

    loads = [
        pltpu.make_async_copy(src, dst, sem_in.at[i])
        for i, (src, dst) in enumerate(
            (
                (ids_hbm, ids_t), (prob_hbm, prob_t), (codes_hbm, codes), (tok_scale_hbm, tok_scale),
                (grad_hbm, grad_out), (in_scale_hbm, in_scale), (down_scale_hbm, down_scale),
            )
        )
    ]
    for load in loads:
        load.start()
    load_in = pltpu.make_async_copy(w_in, weights.at[pl.ds(0, 2 * HID), :], sem_w.at[0])
    load_down = pltpu.make_async_copy(w_down, weights.at[pl.ds(2 * HID, HID), :], sem_w.at[1])
    load_in.start()
    load_down.start()
    for load in loads[:5]:
        load.wait()

    eye = onehot(iota((TOK, TOK), 0) == iota((TOK, TOK), 1))
    before = onehot(iota((TOK, TOK), 0) < iota((TOK, TOK), 1))
    tok_cols = mm(eye, tok_scale[...], ((1,), (1,)))
    for j in range(WL // BLOCK):
        cols = slice(j * BLOCK, (j + 1) * BLOCK)
        payload[:, cols] = (codes[:, cols].astype(F32) * tok_cols[:, j : j + 1]).astype(BF16)
    payload[:, WL:] = grad_out[...]

    slot = iota((NE * PAD, TOK), 0)
    rel_of = slot >> 4
    r_of = slot & 15
    expert_of = ((y + (rel_of >> 3)) & 3) * NZ + ((z + (rel_of & 7)) & 7)
    weight = jnp.zeros((NE * PAD, TOK), F32)
    for k in range(TOP):
        weight = weight + jnp.where(ids_t[k : k + 1, :] == expert_of, prob_t[k : k + 1, :], 0.0)
    place = jnp.where(weight > 0.0, mm(onehot(weight > 0.0), before, ((1,), (0,))), -1.0)
    pick = onehot(place == r_of.astype(F32))
    rest_of = jnp.where(jnp.logical_and(r_of >= CAP, r_of < PAD - 1), (r_of - CAP) * 4, -8)
    by_token = jnp.where(r_of == PAD - 1, weight, 0.0).astype(BF16)
    for b in range(4):
        cols = slice(b * 256, (b + 1) * 256)
        packed = mm(pick, payload[:, cols], ((1,), (0,)))
        packed = packed + mm(onehot(place == (rest_of + b).astype(F32)), payload[:, OUT_W:], ((1,), (0,)))
        if b == 0:
            widen = onehot(iota((TOK, 256), 0) == iota((TOK, 256), 1))
            packed = packed + mm(by_token, widen, ((1,), (0,)))
        send[:, cols] = packed.astype(BF16)
    recv[0:PAD, :] = send[0:PAD, :]

    pl.semaphore_wait(barrier, NE - 1 + 4)

    def at16(ref, rel):
        return ref.at[pl.ds(pl.multiple_of(rel * PAD, PAD), PAD), :]

    def out_copy(rel):
        return pltpu.make_async_remote_copy(
            src_ref=at16(send, rel), dst_ref=at16(recv, rel), send_sem=a_s.at[rel], recv_sem=a_r.at[rel],
            device_id=(ahead(rel), te), device_id_type=MESH,
        )

    def pass_copy(dy):
        rel = dy * NZ + NZ // 2
        return pltpu.make_async_remote_copy(
            src_ref=at16(send, rel), dst_ref=passing.at[dy - RELAYED[0]],
            send_sem=a_s.at[rel], recv_sem=p_r.at[dy - RELAYED[0]],
            device_id=(ahead(dy * NZ + WAY), te), device_id_type=MESH,
        )

    def pass_on_copy(dy):
        rel = dy * NZ + NZ // 2
        return pltpu.make_async_remote_copy(
            src_ref=passing.at[dy - RELAYED[0]], dst_ref=at16(recv, rel),
            send_sem=p_s.at[dy - RELAYED[0]], recv_sem=a_r.at[rel],
            device_id=(ahead(WAY), te), device_id_type=MESH,
        )

    def back_copy(rel):
        return pltpu.make_async_remote_copy(
            src_ref=at16(back_send, rel), dst_ref=at16(back_recv, rel), send_sem=b_s.at[rel], recv_sem=b_r.at[rel],
            device_id=(behind(rel), te), device_id_type=MESH,
        )

    def cols_of(t):
        return pl.ds(pl.multiple_of(t * WL, BLOCK), WL)

    def window(c, t, first=0, count=CH):
        return rows.at[:, pl.ds(pl.multiple_of(c * CH + first, 16), count), cols_of(t)]

    def own_rows(c):
        return own.at[:, pl.ds(pl.multiple_of(c * CH, 16), CH), :]

    def own_copy(c):
        return pltpu.make_async_copy(own_rows(c), window(c, te), sem_own.at[c])

    def gather_copy(c, k):
        ref, peer = (
            (lambda: window(c, te), t_plus),
            (lambda: window(c, te), t_minus),
            (lambda: window(c, te), t_core),
            (lambda: window(c, t_minus, 0, HALF), t_plus),
            (lambda: window(c, t_plus, HALF, HALF), t_minus),
            (lambda: window(c, t_minus), t_core),
            (lambda: window(c, t_plus), t_core),
            (lambda: window(c, t_far), t_core),
        )[k]
        ref = ref()
        return pltpu.make_async_remote_copy(
            src_ref=own_rows(c) if k < 3 else ref, dst_ref=ref, send_sem=g_s.at[k, c], recv_sem=g_r.at[k, c],
            device_id=(er, peer), device_id_type=MESH,
        )

    to_core = (x_far * 2 + other, x_plus * 2 + other, x_minus * 2 + other, t_core)

    def sum_copy(c, k):
        if k < 4:
            src, dst, peer = parts.at[k, c], core_in.at[k, c], t_core
        elif k == 4:
            src, dst, peer = far_sum.at[c, pl.ds(0, HALF), :], relay_a.at[c], t_plus
        elif k == 5:
            src, dst, peer = far_sum.at[c, pl.ds(HALF, HALF), :], relay_b.at[c], t_minus
        elif k == 6:
            src, dst, peer = plus_sum.at[c], from_minus.at[c], t_plus
        elif k == 7:
            src, dst, peer = minus_sum.at[c], from_plus.at[c], t_minus
        elif k == 8:
            src, dst, peer = gate_own.at[c], gate_core.at[c], t_core
        else:
            src, dst, peer = gate_chip.at[c], gate_in.at[k - 9, c], (t_plus, t_minus, t_far)[k - 9]
        return pltpu.make_async_remote_copy(
            src_ref=src, dst_ref=dst, send_sem=r_s.at[k, c], recv_sem=r_r.at[k, c],
            device_id=(er, peer), device_id_type=MESH,
        )

    def scales_stage():
        for load in loads[5:]:
            load.wait()
        load_in.wait()
        load_down.wait()

        flip = onehot(iota((WIDTH // BLOCK, WIDTH // BLOCK), 0) == iota((WIDTH // BLOCK, WIDTH // BLOCK), 1))
        for part in range(3):
            left = in_scale[part * 40 : (part + 1) * 40, :] if part < 2 else down_scale[...]
            total = jnp.zeros((HID, WIDTH // BLOCK), F32)
            for _ in range(3):
                piece = left.astype(BF16)
                total = total + mm(piece, flip, ((0,), (0,)))
                left = left - piece.astype(F32)
            scales[part * HID : (part + 1) * HID, :] = total

    def scale_stage(c):
        @pl.loop(c * STEPS, (c + 1) * STEPS)
        def _(i):
            at = pl.ds(pl.multiple_of(i * 16, 16), 16)
            scale = scales[at, :]
            for q in range(WIDTH // BLOCK):
                cols = slice(q * BLOCK, (q + 1) * BLOCK)
                weights[at, cols] = (weights[at, cols].astype(F32) * scale[:, q : q + 1]).astype(BF16)

    def prepare_stage():
        ids_col = mm(eye, ids_t[...].astype(F32).astype(BF16), ((1,), (1,))).astype(jnp.int32)
        left = prob_t[...]
        prob_by_token = jnp.zeros((TOK, TOP), F32)
        for _ in range(3):
            piece = left.astype(BF16)
            prob_by_token = prob_by_token + mm(eye, piece, ((1,), (1,)))
            left = left - piece.astype(F32)
        wide = iota((TOK, NE * PAD), 1)
        wide_rel = wide >> 4
        wide_r = wide & 15
        wide_expert = ((y + (wide_rel >> 3)) & 3) * NZ + ((z + (wide_rel & 7)) & 7)
        weight = jnp.zeros((TOK, NE * PAD), F32)
        for k in range(TOP):
            weight = weight + jnp.where(ids_col[:, k : k + 1] == wide_expert, prob_by_token[:, k : k + 1], 0.0)
        earlier = onehot(iota((TOK, TOK), 1) < iota((TOK, TOK), 0))
        place = jnp.where(weight > 0.0, mm(earlier, onehot(weight > 0.0), ((1,), (0,))), -1.0)
        rest = jnp.where(jnp.logical_and(wide_r >= CAP, wide_r < PAD - 1), (wide_r - CAP) * 4, -8)
        for b in range(5):
            here = wide_r if b == 4 else rest + b
            kept = jnp.where(place == here.astype(F32), weight, 0.0)
            high = kept.astype(BF16)
            chosen[b, 0:TOK, :] = high
            chosen[b, TOK:, :] = (kept - high.astype(F32)).astype(BF16)
        lane = iota((TOK, 128), 1)
        for k in range(TOP):
            expert = ids_col[:, k : k + 1]
            rel = (((expert >> 3) - y) & 3) * NZ + (((expert & 7) - z) & 7)
            row = wide == rel * PAD + PAD - 1
            gate_pick[k * TOK : (k + 1) * TOK, :] = onehot(row)
            position = jnp.sum(jnp.where(row, place, 0.0), axis=1, keepdims=True)
            spot = ((rel & 7) * CAP).astype(F32) + position
            gate_spot[k * TOK : (k + 1) * TOK, :] = onehot(lane.astype(F32) == spot)

    def far_first(c, i):
        half = i // 2
        return c * NZ + (NZ // 2 + half - (i % 2) * (2 * half + 1) + NZ) % NZ

    def send_stage(c):
        @pl.loop(0, NZ)
        def _(i):
            rel = far_first(c, i)
            relayed = jnp.logical_and(rel >= RELAYED[0] * NZ, lax.rem(rel, NZ) == NZ // 2)

            @pl.when(jnp.logical_and(rel > 0, jnp.logical_not(relayed)))
            def _():
                out_copy(rel).start()

        for dy in RELAYED:

            @pl.when(c == dy - 1)
            def _():
                pass_copy(dy).start()

    def sent_stage(c):
        @pl.loop(0, NZ)
        def _(i):
            rel = c * NZ + i
            relayed = jnp.logical_and(rel >= RELAYED[0] * NZ, i == NZ // 2)

            @pl.when(jnp.logical_and(rel > 0, jnp.logical_not(relayed)))
            def _():
                out_copy(rel).wait_send()

    send_stage(0)

    def dispatch_stage(c):
        sent_stage(c)

        @pl.when(c < NY - 1)
        def _():
            send_stage(c + 1)

        @pl.loop(0, NZ)
        def _(i):
            rel = c * NZ + i

            @pl.when(rel > 0)
            def _():
                out_copy(rel).wait_recv()

        row = iota((CH, CHP), 0)
        col = iota((CH, CHP), 1)
        group = lax.div(row, CAP)
        within = row - group * CAP
        squeeze = onehot(col == group * PAD + within)
        span = pl.ds(pl.multiple_of(c * CH, 16), CH)
        part = pl.ds(pl.multiple_of(c * CHP, CHP), CHP)
        own[0, span, :] = mm(squeeze, recv[part, :WL], ((1,), (0,))).astype(BF16)
        own[1, span, 0 : OUT_W - WL] = mm(squeeze, recv[part, WL:OUT_W], ((1,), (0,))).astype(BF16)
        rest = jnp.zeros((CH, 256), F32)
        for b in range(4):
            here = jnp.logical_and(col == group * PAD + CAP + (within >> 2), (within & 3) == b)
            rest = rest + mm(onehot(here), recv[part, b * 256 : (b + 1) * 256], ((1,), (0,)))
        own[1, span, OUT_W - WL :] = rest.astype(BF16)
        own_copy(c).start()
        for k in (0, 1, 2):
            gather_copy(c, k).start()
        named = mm(onehot(col == group * PAD + PAD - 1), recv[part, :BLOCK], ((1,), (0,)))[:, :TOK]
        rank = mm(onehot(named > 0.0), before, ((1,), (0,)))
        taken = jnp.logical_and(named > 0.0, rank == within[:, :TOK].astype(F32))
        prob_col[span, :] = jnp.sum(jnp.where(taken, named, 0.0), axis=1, keepdims=True)

        for dy in RELAYED:

            @pl.when(c == dy - 1)
            def _():
                pass_copy(dy).wait_recv()
                pass_on_copy(dy).start()

        @pl.when(c == 0)
        def _():
            scales_stage()

        scale_stage(c)

    def relay_stage(c):
        gather_copy(c, 0).wait_recv()
        gather_copy(c, 3).start()
        gather_copy(c, 5).start()
        gather_copy(c, 1).wait_recv()
        gather_copy(c, 4).start()
        gather_copy(c, 6).start()

    def far_stage(c):
        gather_copy(c, 3).wait_recv()
        gather_copy(c, 4).wait_recv()
        gather_copy(c, 7).start()

    def compute_stage(c):
        for k in (2, 5, 6, 7):
            gather_copy(c, k).wait_recv()
        own_copy(c).wait()
        span = pl.ds(pl.multiple_of(c * CH, 16), CH)
        row_values = rows[0, span, :]
        gate = mm(row_values, weights[0:HID, :], ((1,), (1,)))
        up = mm(row_values, weights[HID : 2 * HID, :], ((1,), (1,)))
        hidden = mm(rows[1, span, :], weights[2 * HID :, :], ((1,), (1,)))
        sig = jax.nn.sigmoid(gate)
        act = gate * sig
        gate_full = hidden * up * sig * (1.0 + gate * (1.0 - sig))
        up_full = hidden * act
        gate_grad = gate_full.astype(BF16)
        up_grad = up_full.astype(BF16)
        acted = act * up
        for k in range(8):
            t = (to_core + (t_far, t_plus, t_minus, te))[k]
            part = mm(gate_grad, weights[0:HID, cols_of(t)], ((1,), (0,)))
            part = part + mm(up_grad, weights[HID : 2 * HID, cols_of(t)], ((1,), (0,)))
            if k < 4:
                parts[k, c] = part.astype(BF16)
                sum_copy(c, k).start()
            else:
                kept_parts[k - 4, c] = part.astype(BF16)
        share = hidden * acted
        ones = jnp.ones((8, HID), BF16)
        gate_row = jnp.zeros((8, CH), F32)
        for _ in range(3):
            piece = share.astype(BF16)
            gate_row = gate_row + mm(ones, piece, ((1,), (1,)))
            share = share - piece.astype(F32)
        gate_own[c] = jnp.concatenate([gate_row, jnp.zeros((8, 128 - CH), F32)], axis=1)
        sum_copy(c, 8).start()
        prob = prob_col[span, :]
        hid[0, span, :] = (prob * gate_full).astype(BF16)
        hid[1, span, :] = (prob * up_full).astype(BF16)
        hid[2, span, :] = (prob * acted).astype(BF16)

    def chip_sum(c, k):
        return kept_parts[k, c].astype(F32) + core_in[k, c].astype(F32)

    def core_stage(c):
        sum_copy(c, 0).wait_recv()
        far_sum[c] = chip_sum(c, 0).astype(BF16)
        sum_copy(c, 4).start()
        sum_copy(c, 5).start()
        sum_copy(c, 8).wait_recv()
        gate_chip[c] = gate_own[c] + gate_core[c]
        for k in (9, 10, 11):
            sum_copy(c, k).start()

    def ring_stage(c):
        sum_copy(c, 1).wait_recv()
        total = chip_sum(c, 1)
        sum_copy(c, 4).wait_recv()
        plus_sum[c, 0:HALF, :] = (total[0:HALF] + relay_a[c].astype(F32)).astype(BF16)
        plus_sum[c, HALF:CH, :] = total[HALF:CH].astype(BF16)
        sum_copy(c, 6).start()
        sum_copy(c, 2).wait_recv()
        total = chip_sum(c, 2)
        sum_copy(c, 5).wait_recv()
        minus_sum[c, 0:HALF, :] = total[0:HALF].astype(BF16)
        minus_sum[c, HALF:CH, :] = (total[HALF:CH] + relay_b[c].astype(F32)).astype(BF16)
        sum_copy(c, 7).start()

    def return_stage(c):
        sum_copy(c, 3).wait_recv()
        total = chip_sum(c, 3)
        sum_copy(c, 6).wait_recv()
        sum_copy(c, 7).wait_recv()
        for k in (9, 10, 11):
            sum_copy(c, k).wait_recv()
        gate_row = (gate_chip[c] + gate_in[2, c]) + (gate_in[0, c] + gate_in[1, c])
        total = total + from_minus[c].astype(F32) + from_plus[c].astype(F32)
        row = iota((CHP, CH), 0)
        col = iota((CHP, CH), 1)
        r = row & 15
        first = (row >> 4) * CAP
        spread = onehot(jnp.logical_and(r < CAP, col == first + r))
        extra = jnp.logical_and(r >= CAP, r < PAD - 1)
        values = total.astype(BF16)
        at = pl.ds(pl.multiple_of(c * CHP, CHP), CHP)
        for b in range(4):
            out = mm(spread, values[:, b * 128 : (b + 1) * 128], ((1,), (0,)))
            there = onehot(jnp.logical_and(extra, col == first + (r - CAP) * 4 + b))
            out = out + mm(there, values[:, BACK_W:], ((1,), (0,)))
            if b == 0:
                out = out + jnp.where(iota((CHP, 128), 0) & 15 == PAD - 1, gate_row[0:1, :], 0.0)
            back_send[at, b * 128 : (b + 1) * 128] = out.astype(BF16)

        @pl.loop(0, NZ)
        def _(i):
            rel = far_first(c, i)

            @pl.when(rel > 0)
            def _():
                back_copy(rel).start()

    stages = (
        (dispatch_stage, 0), (relay_stage, 1), (far_stage, 2), (compute_stage, 3),
        (core_stage, 4), (ring_stage, 5), (return_stage, 6),
    )

    @pl.loop(0, NY + 6)
    def _(s):
        for stage, lag in stages:

            @pl.when(jnp.logical_and(s >= lag, s < NY + lag))
            def _():
                stage(s - lag)

        @pl.when(s == NY)
        def _():
            prepare_stage()

        for k in range(3):

            @pl.when(s == NY + 2 + k)
            def _():
                turned = hid[k].T
                for i in range(WIDTH // STEP):
                    cols = slice(i * STEP, (i + 1) * STEP)
                    grads[k, :, cols] = mm(turned, rows[k // 2, :, cols], ((1,), (0,))).astype(BF16)

    back_recv[0:PAD, :] = back_send[0:PAD, :]
    for dy in RELAYED:
        pass_copy(dy).wait_send()
        pass_on_copy(dy).wait_send()

    @pl.loop(0, NY)
    def _(c):
        for k in range(8):
            gather_copy(c, k).wait_send()
        for k in range(12):
            sum_copy(c, k).wait_send()

    @pl.loop(1, NE)
    def _(rel):
        back_copy(rel).wait_send()
        back_copy(rel).wait_recv()

    total = mm(chosen[4], back_recv[...], ((1,), (0,)))
    gi_out[:, 0:BACK_W] = (total[0:TOK] + total[TOK:]).astype(BF16)
    total = jnp.zeros((2 * TOK, 128), F32)
    for b in range(4):
        total = total + mm(chosen[b], back_recv[:, b * 128 : (b + 1) * 128], ((1,), (0,)))
    gi_out[:, BACK_W:] = (total[0:TOK] + total[TOK:]).astype(BF16)
    line = mm(gate_pick[...], back_recv[:, 0:128], ((1,), (0,)))
    line = (line * gate_spot[...].astype(F32)).astype(BF16)
    line = mm(jnp.ones((TOP, 128), BF16), line, ((1,), (1,)))
    at_k = iota((TOP, TOP * TOK), 1) >> 5 == iota((TOP, TOP * TOK), 0)
    at_t = iota((TOP * TOK, TOK), 0) & 31 == iota((TOP * TOK, TOK), 1)
    gg_out[...] = mm(jnp.where(at_k, line, 0.0).astype(BF16), onehot(at_t), ((1,), (0,))).astype(BF16)


def put_grads(grads, gi, gg, grad_in, grad_down, gi_out, gg_out, sems, small):
    copies = [
        pltpu.make_async_copy(
            grads.at[k, pl.ds(i * PART, PART), :],
            (grad_down.at[0] if k == 2 else grad_in.at[0, k]).at[pl.ds(i * PART, PART), :],
            sems.at[k, i],
        )
        for k in range(3)
        for i in range(HID // PART)
    ]
    copies += [pltpu.make_async_copy(gi, gi_out, small.at[0]), pltpu.make_async_copy(gg, gg_out, small.at[1])]
    for copy in copies:
        copy.start()
    for copy in copies:
        copy.wait()


def on_device(
    token_codes, token_scale, grad_out, expert_ids, gate_probs, w_in, w_in_scale, w_down, w_down_scale
):
    vmem = pl.BlockSpec(memory_space=pltpu.VMEM)
    hbm = pl.BlockSpec(memory_space=pl.ANY)
    dma = pltpu.SemaphoreType.DMA
    input_sum, gate_sum, grads = pl.pallas_call(
        exchange,
        out_shape=(
            pltpu.VMEM((TOK, WL), BF16),
            pltpu.VMEM((TOP, TOK), BF16),
            pltpu.VMEM((3, HID, WIDTH), BF16),
        ),
        in_specs=[hbm] * 9,
        out_specs=(vmem, vmem, vmem),
        scratch_shapes=[
            pltpu.VMEM((2, ROWS, WIDTH), BF16),
            pltpu.VMEM((TOP, TOK), jnp.int32),
            pltpu.VMEM((TOP, TOK), F32),
            pltpu.VMEM((TOK, WL), BF16),
            pltpu.VMEM((WL // BLOCK, TOK), BF16),
            pltpu.VMEM((TOK, WL), BF16),
            pltpu.VMEM((2 * (WIDTH // BLOCK), HID), F32),
            pltpu.VMEM((WIDTH // BLOCK, HID), F32),
            pltpu.VMEM((TOK, 2 * WL), BF16),
            pltpu.VMEM((3 * HID, WIDTH // BLOCK), F32),
            pltpu.VMEM((NE * PAD, OUT_W), BF16),
            pltpu.VMEM((NE * PAD, OUT_W), BF16),
            pltpu.VMEM((len(RELAYED), PAD, OUT_W), BF16),
            pltpu.VMEM((2, ROWS, WL), BF16),
            pltpu.VMEM((3 * HID, WIDTH), BF16),
            pltpu.VMEM((4, NY, CH, WL), BF16),
            pltpu.VMEM((4, NY, CH, WL), BF16),
            pltpu.VMEM((4, NY, CH, WL), BF16),
            pltpu.VMEM((NY, 8, 128), F32),
            pltpu.VMEM((NY, 8, 128), F32),
            pltpu.VMEM((NY, 8, 128), F32),
            pltpu.VMEM((3, NY, 8, 128), F32),
            pltpu.VMEM((3, ROWS, HID), BF16),
            pltpu.VMEM((NY, CH, WL), BF16),
            pltpu.VMEM((NY, CH, WL), BF16),
            pltpu.VMEM((NY, CH, WL), BF16),
            pltpu.VMEM((NY, HALF, WL), BF16),
            pltpu.VMEM((NY, HALF, WL), BF16),
            pltpu.VMEM((NY, CH, WL), BF16),
            pltpu.VMEM((NY, CH, WL), BF16),
            pltpu.VMEM((NE * PAD, BACK_W), BF16),
            pltpu.VMEM((NE * PAD, BACK_W), BF16),
            pltpu.VMEM((5, 2 * TOK, NE * PAD), BF16),
            pltpu.VMEM((TOP * TOK, NE * PAD), BF16),
            pltpu.VMEM((TOP * TOK, 128), BF16),
            pltpu.VMEM((ROWS, 1), F32),
            dma((7,)),
            dma((2,)),
            dma((NY,)),
            dma((NE,)),
            dma((NE,)),
            dma((len(RELAYED),)),
            dma((len(RELAYED),)),
            dma((8, NY)),
            dma((8, NY)),
            dma((12, NY)),
            dma((12, NY)),
            dma((NE,)),
            dma((NE,)),
        ],
        compiler_params=pltpu.CompilerParams(
            collective_id=0, has_side_effects=True, vmem_limit_bytes=52 * 1024 * 1024
        ),
    )(
        expert_ids.T, gate_probs.T, token_codes, token_scale.T, grad_out,
        w_in_scale.transpose(0, 1, 3, 2).reshape(2 * (WIDTH // BLOCK), HID),
        w_down_scale.transpose(0, 2, 1).reshape(WIDTH // BLOCK, HID),
        w_in.reshape(2 * HID, WIDTH), w_down.reshape(HID, WIDTH),
    )
    grad_w_in, grad_w_down, grad_input, grad_gates = pl.pallas_call(
        put_grads,
        in_specs=[vmem] * 3,
        out_specs=(hbm,) * 4,
        out_shape=(
            jax.ShapeDtypeStruct((1, 2, HID, WIDTH), BF16),
            jax.ShapeDtypeStruct((1, HID, WIDTH), BF16),
            jax.ShapeDtypeStruct((TOK, WL), BF16),
            jax.ShapeDtypeStruct((TOP, TOK), BF16),
        ),
        scratch_shapes=[dma((3, HID // PART)), dma((2,))],
        compiler_params=pltpu.CompilerParams(vmem_limit_bytes=8 * 1024 * 1024),
    )(grads, input_sum, gate_sum)
    return (grad_input, grad_gates.T, grad_w_in, grad_w_down)


def solution(mesh):
    placed = (
        P("expert", "tensor"),
        P("expert", "tensor"),
        P("expert", "tensor"),
        P("expert", None),
        P("expert", None),
        P("expert", None, "tensor", None),
        P("expert", None, "tensor", None),
        P("expert", "tensor", None),
        P("expert", "tensor", None),
    )
    return jax.shard_map(
        on_device,
        mesh=mesh,
        in_specs=placed,
        out_specs=(
            P("expert", "tensor"),
            P("expert", None),
            P("expert", None, "tensor", None),
            P("expert", "tensor", None),
        ),
        check_vma=False,
    )
```
